256 devices in a mesh: blk: 8 (over x, y_hi), rep: 8 (over z), feat: 4 (over y_lo, core).
Axes of the slice: x: 4, y: 4 (y_hi: 2, y_lo: 2; y = y_hi * 2 + y_lo), z: 8, core: 2. Of those that a mesh axis runs over, the one named last changes fastest.
Arguments:
- features: bfloat16 [16384, 128], P(('blk', 'rep')), may hold values from -6 to 6
- weight_in: bfloat16 [128, 512], P(None, 'feat'), may hold values from -0.5 to 0.5
- bias_in: float32 [512], P('feat'), may hold values from -3 to 3
- weight_mid: bfloat16 [512, 512], P(None, 'feat'), may hold values from -0.25 to 0.25
- bias_mid: float32 [512], P('feat'), may hold values from -3 to 3
- light_tiles: bfloat16 [64, 8, 36, 128, 128], P(('blk', 'rep')), may hold values from -0.046875 to 0.046875
- light_rows: int32 [64, 8, 36], P(('blk', 'rep')), may hold values from 0 to 1
- light_cols: int32 [64, 8, 36], P(('blk', 'rep')), may hold values from 0 to 15
- heavy_tiles: bfloat16 [64, 8, 8, 128, 128], P(('blk', 'rep')), may hold values from -0.0625 to 0.0625
- heavy_slots: int32 [64, 8, 8], P(('blk', 'rep')), may hold values from 0 to 63, all different within a row; in each aligned block of 8 rows (0 to 7, 8 to 15, ..., all dimensions but the last counted through in order) at most 2 rows name the same one
- heavy_cols: int32 [64, 8, 8], P(('blk', 'rep')), may hold values from 0 to 15
- owner_map: int32 [64], P(('blk', 'rep')), may hold values from 0 to 1
Outputs:
- output: bfloat16 [16384, 512], P(('blk', 'rep'), 'feat')
The draws below stay inside these ranges and needn't reach their ends.
Inputs may be any that keep to these rules, and one draw needn't show every extreme that they name: `heavy_slots`: the 8 heavy tiles of one group and source step name distinct heavy tile rows; among the 64 heavy tiles of one group no heavy tile row is named more than 2 times, and some row is named exactly that often. How many heavy tiles add to one heavy tile row in all differs from row to row.
All inputs are finite; a program needn't handle non-finite values.
Results may differ from the reference program's by a relative error of at most 0.0065.
Values may be sent and summed in bfloat16 or wider, within the bound.
No kernel may reach another device: no remote copies, remote signals or barrier semaphores. Data moves between devices by JAX's collectives and lax.ppermute only.
A program may use at most 192 MiB of HBM per device.

```python
import math
import jax
import jax.numpy as jnp
import numpy as np
from jax import lax

F_IN = 128
HID = 512
TILE = 128
ROW_TILES = 2
LT = 36
HT = 8
SLOT_MOST = 2
GROUPS = 64
COL_TILES = 16
NODES = 16384
N_BLK = 8
N_REP = 8


def place_ends(entries, key, smallest, largest):
    extent = entries.shape
    place = [jax.random.randint(jax.random.fold_in(key, axis), (), 0, extent[axis]) for axis in range(len(extent))]
    entries = entries.at[tuple(place)].set(smallest)
    longest = extent.index(max(extent))
    place[longest] = (place[longest] + 1) % extent[longest]
    return entries.at[tuple(place)].set(largest)


def block_levels(own_key, dims, cuts, smallest, high):
    loudness = 1.0
    for position, shards_of in cuts:
        heights = jax.random.uniform(jax.random.fold_in(jax.random.fold_in(own_key, 6), position), (shards_of,), jnp.float32, smallest / len(cuts), high / len(cuts))
        loudness = loudness * jnp.repeat(jnp.exp(heights), dims[position] // shards_of).reshape((-1,) + (1,) * (len(dims) - 1 - position))
    return loudness


def assign_block(rng, own, number, rows, number_of, top, bound, slope):
    order = jax.random.permutation(rng, number_of)
    crowded, ordinary = portions_of(number_of, rows * top, bound, slope, True), portions_of(number_of, rows * top, bound, slope, False)
    places = jnp.arange(number_of)

    def named(sizes, offset_by):
        used = int((sizes > 0).sum())
        fixed = max(1, used // 4)
        moved = fixed + (places - fixed + offset_by * (used - fixed)) % max(1, number_of - fixed)
        return jnp.zeros((number_of,), jnp.int32).at[order[jnp.where(places < fixed, places, moved)]].set(jnp.asarray(sizes, jnp.int32))

    sizes = jnp.where(number % 4 == 0, named(crowded, number // 4), named(ordinary, number - number // 4 - 1))
    mixed = jax.random.permutation(jax.random.fold_in(own, 3), number_of)
    donor, receiver = mixed[0:number_of // 2 * 2:2], mixed[1:number_of // 2 * 2:2]
    room = jnp.minimum(sizes[donor] - 1, bound - sizes[receiver]) // 2
    room = jnp.where((donor == order[0]) | (receiver == order[0]) | (sizes[receiver] == 0), 0, jnp.maximum(room, 0))
    moved = jax.random.randint(jax.random.fold_in(own, 4), (number_of // 2,), 0, 1 << 20) % (room + 1)
    sizes = sizes.at[donor].add(-moved).at[receiver].add(moved)
    members = jnp.searchsorted(jnp.cumsum(sizes), jnp.arange(rows * top), side="right").astype(jnp.int32)
    listing = members.reshape(top, rows).T
    listing = listing[jax.random.permutation(jax.random.fold_in(own, 1), rows)]
    offset_by = jax.random.randint(jax.random.fold_in(own, 2), (rows, 1), 0, top)
    return jnp.take_along_axis(listing, (jnp.arange(top)[None, :] + offset_by) % top, axis=1)


def portions_of(amount, total, bound, slope, full):
    weights = [(1 << 20) // math.isqrt(standing ** slope) + 1 for standing in range(1, amount + 1)]
    largest = bound if full else min(bound, max(-(-total // amount), total * weights[0] // sum(weights)))
    least = 1 if total - largest >= amount - 1 else 0
    holding, rest = [largest] + [least] * (amount - 1), total - largest - least * (amount - 1)
    while rest > 0:
        free = [i for i in range(1, amount) if holding[i] < largest] or [i for i in range(1, amount) if holding[i] < bound]
        pool, remaining = sum([weights[i] for i in free]), rest
        for i in free:
            addition = min(bound - holding[i], max(1, remaining * weights[i] // pool), rest)
            holding[i] = holding[i] + addition
            rest = rest - addition
    return np.array(holding)


def bell_draw(stream_key, dims, scale, bound, split=(), kind=jnp.bfloat16):
    drawn = scale * jax.random.normal(stream_key, dims, jnp.float32)
    if split:
        drawn = drawn * block_levels(stream_key, dims, split, -0.22, 0.18)
    return jnp.clip(drawn, -bound, bound).astype(kind)


def setup_inputs(seed: int = 0) -> dict:
    splits = jax.random.split(jax.random.key(seed), 13)
    features = bell_draw(splits[0], (NODES, F_IN), 1.0, 6.0, ((0, 64),))
    weight_in = bell_draw(splits[1], (F_IN, HID), F_IN ** -0.5, 0.5, ((1, 4),))
    bias_in = bell_draw(splits[2], (HID,), 0.5, 3.0, ((0, 4),), jnp.float32)
    weight_mid = bell_draw(splits[3], (HID, HID), HID ** -0.5, 0.25, ((1, 4),))
    bias_mid = bell_draw(splits[4], (HID,), 0.5, 3.0, ((0, 4),), jnp.float32)
    light_tiles = bell_draw(splits[5], (GROUPS, N_BLK, LT, TILE, TILE), (TILE * LT * N_BLK // ROW_TILES) ** -0.5, 0.046875, ((0, 64),))
    light_rows = place_ends(jax.random.randint(splits[6], (GROUPS, N_BLK, LT), 0, ROW_TILES), jax.random.fold_in(splits[6], 1), 0, ROW_TILES - 1).astype(jnp.int32)
    light_cols = place_ends(jax.random.randint(splits[7], (GROUPS, N_BLK, LT), 0, COL_TILES), jax.random.fold_in(splits[7], 1), 0, COL_TILES - 1).astype(jnp.int32)
    heavy_tiles = bell_draw(splits[8], (GROUPS, N_BLK, HT, TILE, TILE), (TILE * HT * N_BLK) ** -0.5, 0.0625, ((0, 64),))
    heavy_slots_keys = jax.random.split(jax.random.fold_in(splits[9], 1), GROUPS * N_BLK // N_BLK)
    heavy_slots_turns = jax.random.permutation(jax.random.fold_in(splits[9], 3), GROUPS * N_BLK // N_BLK)
    heavy_slots = jax.vmap(lambda own, number: assign_block(jax.random.fold_in(splits[9], 2), own, number, N_BLK, GROUPS, HT, SLOT_MOST, 2))(heavy_slots_keys, heavy_slots_turns).reshape((GROUPS, N_BLK, HT))
    heavy_cols = place_ends(jax.random.randint(splits[10], (GROUPS, N_BLK, HT), 0, COL_TILES), jax.random.fold_in(splits[10], 1), 0, COL_TILES - 1).astype(jnp.int32)
    owner_map = place_ends(jax.random.randint(splits[11], (GROUPS,), 0, ROW_TILES), jax.random.fold_in(splits[11], 1), 0, ROW_TILES - 1).astype(jnp.int32)
    return dict(features=features, weight_in=weight_in, bias_in=bias_in, weight_mid=weight_mid, bias_mid=bias_mid, light_tiles=light_tiles, light_rows=light_rows, light_cols=light_cols, heavy_tiles=heavy_tiles, heavy_slots=heavy_slots, heavy_cols=heavy_cols, owner_map=owner_map)


def aggregate(values, light_tiles, light_rows, light_cols, heavy_tiles, heavy_slots, heavy_cols, owner_map):
    width = values.shape[1]
    blocks = values.reshape(N_BLK, N_REP * ROW_TILES, TILE, width)
    steps_idx = jnp.arange(N_BLK, dtype=jnp.int32)
    row_ids = jnp.arange(ROW_TILES, dtype=jnp.int32)
    group_ids = jnp.arange(GROUPS, dtype=jnp.int32)

    def one_group(carry, inputs):
        group, tiles, rows, cols, htiles, slots, hcols = inputs
        source = (group // N_REP - steps_idx) % N_BLK
        picked = blocks[source[:, None], cols].astype(jnp.float32)
        products = jnp.einsum("skij,skjf->skif", tiles.astype(jnp.float32), picked, precision=lax.Precision.HIGHEST)
        onehot = (rows[..., None] == row_ids).astype(jnp.float32)
        light = jnp.einsum("skt,skif->tif", onehot, products, precision=lax.Precision.HIGHEST)
        hpicked = blocks[source[:, None], hcols].astype(jnp.float32)
        hproducts = jnp.einsum("skij,skjf->skif", htiles.astype(jnp.float32), hpicked, precision=lax.Precision.HIGHEST)
        honehot = (slots[..., None] == group_ids).astype(jnp.float32)
        carry = carry + jnp.einsum("skq,skif->qif", honehot, hproducts, precision=lax.Precision.HIGHEST)
        return carry, light

    start = jnp.zeros((GROUPS, TILE, width), jnp.float32)
    heavy, light = lax.scan(one_group, start, (group_ids, light_tiles, light_rows, light_cols, heavy_tiles, heavy_slots, heavy_cols))
    owners = (owner_map[:, None] == row_ids[None, :]).astype(jnp.float32)
    total = light + owners[:, :, None, None] * heavy[:, None, :, :]
    return total.reshape(NODES, width)


def reference(features, weight_in, bias_in, weight_mid, bias_mid, light_tiles, light_rows, light_cols, heavy_tiles, heavy_slots, heavy_cols, owner_map):
    graph = (light_tiles, light_rows, light_cols, heavy_tiles, heavy_slots, heavy_cols, owner_map)
    first = jnp.dot(features, weight_in, preferred_element_type=jnp.float32).astype(jnp.bfloat16)
    hidden = jnp.maximum(aggregate(first, *graph) + bias_in, 0.0).astype(jnp.bfloat16)
    second = jnp.dot(hidden, weight_mid, preferred_element_type=jnp.float32).astype(jnp.bfloat16)
    return (aggregate(second, *graph) + bias_mid).astype(jnp.bfloat16)
```

```python
import jax
import jax.numpy as jnp
from jax import lax
from jax.experimental import pallas as pl
from jax.experimental.pallas import tpu as pltpu
from jax.sharding import Mesh
from jax.sharding import PartitionSpec as P

BLK = ("x", "yh")
GROUP = ("x", "yh", "z")
FEAT = ("yl", "c")
PLANE = ("yh", "z")
T = 128
NB = 8
NR = 8
NG = NB * NR
NT = 2 * NG
LT = 36
HT = 8
NL = NB * LT
NH = NB * HT
SLOTS = 2 * NG
QR = T // 4
STEP = 16
NOTES = 8
CHUNKS = 4
CHUNK_STEPS = NB // CHUNKS
CHUNK = CHUNK_STEPS * LT
NX = 4
NPLANE = 2 * NR
HSTEP = 32
HELD = ((0, NPLANE), (NPLANE, NPLANE), (3 * NPLANE, NPLANE), (2 * NPLANE, NR), (2 * NPLANE + NR, NR))
BF16 = jnp.bfloat16
SMEM = pl.BlockSpec(memory_space=pltpu.SMEM)
VMEM = pl.BlockSpec(memory_space=pltpu.VMEM)
ANY = pl.BlockSpec(memory_space=pl.ANY)


def params(mib):
    return pltpu.CompilerParams(vmem_limit_bytes=mib * 1024 * 1024)


def turned(blk, source):
    return (((blk >> 1) - (source >> 1)) & 3) * 2 + (source & 1)


def around(axis, distance):
    n = lax.axis_size(axis)
    return [(i, (i + distance) % n) for i in range(n)]


def along_x(near):
    behind = lax.ppermute(near, "x", around("x", 1))
    ahead = lax.ppermute(near, "x", around("x", -1))
    far = near.shape[0] // 2
    return [
        near,
        behind,
        ahead,
        lax.ppermute(behind[:far], "x", around("x", 1)),
        lax.ppermute(ahead[far:], "x", around("x", -1)),
    ]


def swap(x, axis):
    return lax.ppermute(x, axis, around(axis, 1))


def everyone(x, axis, n):
    spread = jnp.broadcast_to(x[None], (n, *x.shape))
    return lax.all_to_all(spread, axis, 0, 0, tiled=True)


def pack_kernel(
    meta, slots, cols, rows, lcols, heavy, out, ids, places, need, trips, quarter, seats, taken, sem
):
    blk, feat = meta[0], meta[1]
    span = pl.ds(pl.multiple_of(feat * QR, QR), QR)
    copy = pltpu.make_async_copy(heavy.at[:, span, :], quarter.at[pl.ds(0, NH)], sem)
    copy.start()
    quarter[NH] = jnp.zeros((QR, T), BF16)

    def clear(q, carry):
        taken[q] = 0
        seats[2 * q] = NH
        seats[2 * q + 1] = NH
        return carry

    lax.fori_loop(0, NG, clear, 0, unroll=8)

    def seat(i, carry):
        q = slots[0, i // HT, i % HT]
        turn = taken[q]
        taken[q] = turn + 1
        seats[2 * q + turn] = i
        return carry

    lax.fori_loop(0, NH, seat, 0, unroll=8)
    lane = lax.broadcasted_iota(jnp.int32, (NOTES, T), 1)
    copy.wait()

    def node(i):
        j = jnp.minimum(i, NH - 1)
        tile = ((blk - (j >> 3)) & (NB - 1)) * 2 * NR + cols[0, j >> 3, j & (HT - 1)]
        return jnp.where(i < NH, tile, NT)

    def fill(q, carry):
        a, b = seats[2 * q], seats[2 * q + 1]
        notes = jnp.where(lane == 0, node(a), node(b)).astype(jnp.float32).astype(BF16)
        out[q] = jnp.concatenate([quarter[a], quarter[b], notes], axis=0)
        return carry

    lax.fori_loop(0, NG, fill, 0, unroll=4)

    def clear_lists(i, carry):
        for t in range(2):
            ids[t, i] = 0
            places[t, i] = NT
        return carry

    lax.fori_loop(0, NL, clear_lists, 0, unroll=8)
    for g in range(NL // STEP):
        need[g] = 0

    def put(k, carry, s, start):
        n0, n1 = carry
        row, col = rows[0, s, k], lcols[0, s, k]
        at = jnp.where(row == 0, n0, n1)
        ids[row, at] = s * LT + k
        places[row, at] = start + (col & 1) * NG + (col >> 1)
        need[at >> 4] = s // CHUNK_STEPS
        return n0 + 1 - row, n1 + row

    counts = (0, 0)
    for s in range(NB):
        start = turned(blk, (blk - s) & (NB - 1)) * NR
        counts = lax.fori_loop(0, LT, lambda k, c, s=s, v=start: put(k, c, s, v), counts, unroll=6)
    trips[0] = (jnp.maximum(counts[0], counts[1]) + STEP - 1) // STEP


def compact_kernel(hplaces, ids, places, htrips):
    def clear(i, carry):
        ids[i] = 0
        places[i] = NT
        return carry

    lax.fori_loop(0, NL, clear, 0, unroll=8)

    def put(i, n):
        place = hplaces[i]
        ids[n] = i
        places[n] = place
        return n + jnp.where(place < NT, 1, 0)

    n = lax.fori_loop(0, SLOTS, put, 0, unroll=8)
    ids[n] = 0
    places[n] = NT
    htrips[0] = (n + STEP - 1) // STEP


def dots(tile, value, count, ids, places, acc):
    for u in range(0, count, 2):
        left = jnp.concatenate([tile(ids(u)), tile(ids(u + 1))], axis=1)
        right = jnp.concatenate([value(places(u)), value(places(u + 1))], axis=0)
        acc = acc + jnp.dot(left, right, preferred_element_type=jnp.float32)
    return acc


def feature_copies(meta, parts, values, sems):
    core = meta[2]
    copies = []
    for which in range(2):
        c = core if which == 0 else 1 - core
        for (start, size), part in zip(HELD, parts[which * len(HELD) : (which + 1) * len(HELD)]):
            span = pl.ds(c * NG + start, size)
            copies.append(pltpu.make_async_copy(part, values.at[span], sems.at[len(copies)]))
    return copies


def first_kernel(meta, trips, ids, places, hplaces, light, heavy, *rest):
    parts, (out, values, tiles, htiles, sems) = rest[: 2 * len(HELD)], rest[2 * len(HELD) :]
    owner = meta[3]
    rows = pl.ds(pl.multiple_of(meta[1] * QR, QR), QR)
    copies = feature_copies(meta, parts, values, sems)
    copies.append(pltpu.make_async_copy(light.at[:, rows, :], tiles, sems.at[len(copies)]))
    for slot in range(2):
        rows, span = pl.ds(slot * QR, QR), pl.ds(slot * NG, NG)
        copies.append(
            pltpu.make_async_copy(heavy.at[:, rows, :], htiles.at[span], sems.at[len(copies)])
        )
    for copy in copies:
        copy.start()
    values[NT] = jnp.zeros((T, T), BF16)
    for copy in copies:
        copy.wait()
    value = lambda p: values[p]

    def body(g, carry):
        base = g * STEP
        return [
            dots(
                lambda i: tiles[i], value, STEP,
                lambda u: ids[t, base + u], lambda u: places[t, base + u], carry[t],
            )
            for t in range(2)
        ]

    zero = jnp.zeros((QR, T), jnp.float32)
    sums = lax.fori_loop(0, trips[0], body, [zero, zero])

    def heavy_body(g, acc):
        base = g * HSTEP
        return dots(
            lambda i: htiles[i], value, HSTEP,
            lambda u: base + u, lambda u: hplaces[base + u], acc,
        )

    hsum = lax.fori_loop(0, SLOTS // HSTEP, heavy_body, zero)
    for t in range(2):
        out[t] = (sums[t] + jnp.where(owner == t, hsum, 0.0)).astype(BF16)


def project_kernel(gathered, w_in, b_in, w_mid, mine, theirs):
    for rt in range(2):
        x = gathered[:, :, rt].reshape(-1, T)
        h = jnp.dot(x, w_in[...], preferred_element_type=jnp.float32) + b_in[...]
        h = jnp.maximum(h, 0.0).astype(BF16)
        s = jnp.dot(h, w_mid[...], preferred_element_type=jnp.float32).astype(BF16)
        mine[rt] = s[:, :T].reshape(mine.shape[1:])
        theirs[rt] = s[:, T:].reshape(theirs.shape[1:])


def second_kernel(meta, trips, htrips, need, ids, places, hids, hplaces, light, h0, h1, h2, h3, b_mid, *rest):
    parts, (out, values, tiles, htiles, sems, light_sems) = rest[: 2 * len(HELD)], rest[2 * len(HELD) :]
    core, feat, owner = meta[2], meta[1], meta[3]
    copies = []
    for which in range(2):
        c = core if which == 0 else 1 - core
        for (start, size), part in zip(HELD, parts[which * len(HELD) : (which + 1) * len(HELD)]):
            for rt in range(2):
                span = pl.ds(rt * NG + start, size)
                copies.append(
                    pltpu.make_async_copy(part.at[rt], values.at[span, :, c], sems.at[len(copies)])
                )
    first = len(copies)
    for k, h in enumerate((h0, h1, h2, h3)):
        rows = pl.ds(pl.multiple_of((feat ^ k) * QR, QR), QR)
        for slot in range(2):
            copies.append(
                pltpu.make_async_copy(
                    h.at[:, pl.ds(slot * QR, QR), :],
                    htiles.at[pl.ds(slot * NG, NG), rows, :],
                    sems.at[len(copies)],
                )
            )

    def chunk(n):
        span = pl.ds(n * CHUNK, CHUNK)
        return pltpu.make_async_copy(light.at[span], tiles.at[span], light_sems.at[n])

    for copy in copies[:first]:
        copy.start()
    for n in range(CHUNKS):
        chunk(n).start()
    for copy in copies[first:]:
        copy.start()
    values[NT] = jnp.zeros((2, 2, QR, T), BF16)
    for copy in copies[:first]:
        copy.wait()

    def wait_for(n):
        chunk(n).wait()
        return n + 1

    value = lambda p: values[p].reshape(T, T)

    def body(g, carry):
        here = lax.while_loop(lambda n: n <= need[g], wait_for, carry[2])
        base = g * STEP
        sums = [
            dots(
                lambda i: tiles[i], value, STEP,
                lambda u: ids[t, base + u], lambda u: places[t, base + u], carry[t],
            )
            for t in range(2)
        ]
        return (*sums, here)

    zero = jnp.zeros((T, T), jnp.float32)
    sum0, sum1, here = lax.fori_loop(0, trips[0], body, (zero, zero, 0))
    lax.while_loop(lambda n: n < CHUNKS, wait_for, here)
    for copy in copies[first:]:
        copy.wait()

    def heavy_body(g, acc):
        base = g * STEP
        return dots(
            lambda i: htiles[i], value, STEP, lambda u: hids[base + u], lambda u: hplaces[base + u], acc
        )

    hsum = lax.fori_loop(0, htrips[0], heavy_body, zero)
    out[:T] = (sum0 + jnp.where(owner == 0, hsum, 0.0) + b_mid[...]).astype(BF16)
    out[T:] = (sum1 + jnp.where(owner == 1, hsum, 0.0) + b_mid[...]).astype(BF16)


def per_device(
    features, weight_in, bias_in, weight_mid, bias_mid, light_tiles, light_rows, light_cols,
    heavy_tiles, heavy_slots, heavy_cols, owner_map,
):
    i32 = jnp.int32
    blk, core, feat = lax.axis_index(BLK), lax.axis_index("c"), lax.axis_index(FEAT)
    meta = jnp.stack([blk, feat, core, owner_map[0]]).astype(i32)
    light = light_tiles.reshape(NL, T, T)
    int_list = jax.ShapeDtypeStruct((NL,), i32)
    int_lists = jax.ShapeDtypeStruct((2, NL), i32)
    needs = jax.ShapeDtypeStruct((NL // STEP,), i32)
    one_int = jax.ShapeDtypeStruct((1,), i32)

    half = lax.dynamic_slice_in_dim(features, core * T, T, axis=0)
    plane = everyone(half, PLANE, NPLANE)

    packed, ids, places, need, trips = pl.pallas_call(
        pack_kernel,
        out_shape=(
            jax.ShapeDtypeStruct((NG, 2 * QR + NOTES, T), BF16), int_lists, int_lists, needs, one_int
        ),
        in_specs=[SMEM] * 5 + [ANY],
        out_specs=(VMEM, SMEM, SMEM, SMEM, SMEM),
        scratch_shapes=[
            pltpu.VMEM((NH + 1, QR, T), BF16),
            pltpu.SMEM((SLOTS,), i32),
            pltpu.SMEM((NG,), i32),
            pltpu.SemaphoreType.DMA(()),
        ],
        compiler_params=params(16),
        cost_estimate=pl.CostEstimate(flops=0, transcendentals=0, bytes_accessed=30_000_000),
        name="pack",
    )(meta, heavy_slots, heavy_cols, light_rows, light_cols, heavy_tiles.reshape(NH, T, T))
    arrived = lax.all_to_all(packed, GROUP, 0, 0, tiled=True)
    own = along_x(plane)
    held = own + [swap(part, "c") for part in own]

    nodes = arrived[:, 2 * QR, :2].T.reshape(SLOTS).astype(i32)
    hplaces = jnp.where(
        nodes < NT, (nodes & 1) * NG + turned(blk, nodes >> 4) * NR + ((nodes & 15) >> 1), NT
    )

    aggregated = pl.pallas_call(
        first_kernel,
        out_shape=jax.ShapeDtypeStruct((2, QR, T), BF16),
        in_specs=[SMEM] * 5 + [ANY] * (2 + len(held)),
        out_specs=VMEM,
        scratch_shapes=[
            pltpu.VMEM((NT + 1, T, T), BF16),
            pltpu.VMEM((NL, QR, T), BF16),
            pltpu.VMEM((SLOTS, QR, T), BF16),
            pltpu.SemaphoreType.DMA((len(held) + 3,)),
        ],
        compiler_params=params(54),
        name="aggregate_first",
    )(meta, trips, ids, places, hplaces, light, arrived, *held)

    aggregated, weight_in, bias_in, weight_mid = lax.optimization_barrier(
        (aggregated, weight_in, bias_in, weight_mid)
    )
    bias_rows = jnp.pad(bias_in.reshape(1, T), ((0, 7), (0, 0)))
    pieces = jnp.concatenate([weight_in.astype(jnp.float32), bias_rows], axis=0)
    pieces = jnp.stack([pieces, swap(pieces, "yl")])
    pieces = jnp.stack([pieces, swap(pieces, "c")], axis=1).reshape(4, T + 8, T)
    pieces = jnp.take(pieces, feat ^ jnp.arange(4), axis=0)
    w_in = jnp.moveaxis(pieces[:, :T], 0, 1).reshape(T, 4 * T).astype(BF16)
    b_in = pieces[:, T].reshape(1, 4 * T)
    w_mid = jnp.concatenate([weight_mid, swap(weight_mid, "c")], axis=1)

    rows = everyone(aggregated, (*PLANE, "yl"), 2 * NPLANE).reshape(NPLANE, 2, 2, QR, T)

    hids, hlist, htrips = pl.pallas_call(
        compact_kernel,
        out_shape=(int_list, int_list, one_int),
        in_specs=[SMEM],
        out_specs=(SMEM,) * 3,
        name="compact",
    )(hplaces)

    rows, arrived, w_in, b_in, w_mid, hids, hlist, htrips = lax.optimization_barrier(
        (rows, arrived, w_in, b_in, w_mid, hids, hlist, htrips)
    )
    hc = swap(arrived, "c")
    hy = swap(arrived, "yl")
    def project(part):
        half_values = jax.ShapeDtypeStruct((2, part.shape[0], 2, QR, T), BF16)
        return pl.pallas_call(
            project_kernel,
            out_shape=(half_values, half_values),
            in_specs=[VMEM] * 4,
            out_specs=(VMEM, VMEM),
            compiler_params=params(16),
            name="project",
        )(part, w_in, b_in, w_mid)

    behind = lax.ppermute(rows, "x", around("x", 1))
    ahead = lax.ppermute(rows, "x", around("x", -1))
    near = project(rows)
    behind, ahead, near = lax.optimization_barrier((behind, ahead, near))
    far = [
        lax.ppermute(behind[:NR], "x", around("x", 1)),
        lax.ppermute(ahead[NR:], "x", around("x", -1)),
    ]
    sides = [project(behind), project(ahead)]
    swapped = [swap(part[1], "c") for part in [near] + sides]
    far, sides, swapped = lax.optimization_barrier((far, sides, swapped))
    far = [project(part) for part in far]
    swapped += [swap(part[1], "c") for part in far]
    mine = [part[0] for part in [near] + sides + far]
    hy_late, _ = lax.optimization_barrier((hy, far))
    hyc = swap(hy_late, "c")
    return pl.pallas_call(
        second_kernel,
        out_shape=jax.ShapeDtypeStruct((2 * T, T), BF16),
        in_specs=[SMEM] * 8 + [ANY] * 5 + [VMEM] + [ANY] * len(held),
        out_specs=VMEM,
        scratch_shapes=[
            pltpu.VMEM((NT + 1, 2, 2, QR, T), BF16),
            pltpu.VMEM((NL, T, T), BF16),
            pltpu.VMEM((SLOTS, T, T), BF16),
            pltpu.SemaphoreType.DMA((2 * len(held) + 8,)),
            pltpu.SemaphoreType.DMA((CHUNKS,)),
        ],
        compiler_params=params(54),
        name="aggregate_second",
    )(
        meta, trips, htrips, need, ids, places, hids, hlist, light, arrived, hc, hy, hyc,
        bias_mid.reshape(1, T), *mine, *swapped,
    )


def solution(mesh):
    wide = Mesh(mesh.devices.reshape(4, 2, 8, 2, 2), ("x", "yh", "z", "yl", "c"))
    in_specs = (
        P(GROUP, None),
        P(None, FEAT),
        P(FEAT),
        P(None, FEAT),
        P(FEAT),
        P(GROUP, None, None, None, None),
        P(GROUP, None, None),
        P(GROUP, None, None),
        P(GROUP, None, None, None, None),
        P(GROUP, None, None),
        P(GROUP, None, None),
        P(GROUP),
    )
    return jax.shard_map(
        per_device, mesh=wide, in_specs=in_specs, out_specs=P(GROUP, FEAT), check_vma=False
    )
```

```python
import functools

import jax
import jax.numpy as jnp
from jax import lax
from jax.experimental import pallas as pl
from jax.experimental.pallas import tpu as pltpu
from jax.sharding import Mesh
from jax.sharding import PartitionSpec as P

BLK = ("x", "yh")
GROUP = ("x", "yh", "z")
FEAT = ("yl", "c")
PLANE = ("yh", "z")
T = 128
NB = 8
NR = 8
NG = NB * NR
NT = 2 * NG
LT = 36
HT = 8
NL = NB * LT
NH = NB * HT
SLOTS = 2 * NG
QR = T // 4
STEP = 16
NOTES = 8
NX = 4
NPLANE = 2 * NR
HSTEP = 32
NEAR_STEPS = NB - 2
FAR_AT = -(-NEAR_STEPS * LT // STEP) * STEP
LIST = FAR_AT + -(-2 * LT // STEP) * STEP
HELD = ((0, NPLANE), (NPLANE, NPLANE), (3 * NPLANE, NPLANE), (2 * NPLANE, NR), (2 * NPLANE + NR, NR))
BF16 = jnp.bfloat16
SMEM = pl.BlockSpec(memory_space=pltpu.SMEM)
VMEM = pl.BlockSpec(memory_space=pltpu.VMEM)
ANY = pl.BlockSpec(memory_space=pl.ANY)


def params(mib):
    return pltpu.CompilerParams(vmem_limit_bytes=mib * 1024 * 1024)


def turned(blk, source):
    return (((blk >> 1) - (source >> 1)) & 3) * 2 + (source & 1)

PROJECTED = ((0, 0, 0, NPLANE), (1, 0, NPLANE, NPLANE), (1, NPLANE, 3 * NPLANE, NPLANE), (2, 0, 2 * NPLANE, NPLANE))


def step_of(blk, j):
    order = j if j < 4 else (j + 2 if j < NEAR_STEPS else j - 2)
    held, y = order >> 1, order & 1
    source = (((blk >> 1) - held) & 3) * 2 + y
    return (blk - source) & (NB - 1), order * NR


def around(axis, distance):
    n = lax.axis_size(axis)
    return [(i, (i + distance) % n) for i in range(n)]


def along_x(near):
    behind = lax.ppermute(near, "x", around("x", 1))
    ahead = lax.ppermute(near, "x", around("x", -1))
    far = near.shape[0] // 2
    return [
        near,
        behind,
        ahead,
        lax.ppermute(behind[:far], "x", around("x", 1)),
        lax.ppermute(ahead[far:], "x", around("x", -1)),
    ]


def swap(x, axis):
    return lax.ppermute(x, axis, around(axis, 1))


def everyone(x, axis, n):
    spread = jnp.broadcast_to(x[None], (n, *x.shape))
    return lax.all_to_all(spread, axis, 0, 0, tiled=True)


def pack_kernel(
    meta, slots, cols, rows, lcols, heavy, out, ids, places, need, trips, quarter, seats, taken, sem
):
    blk, feat = meta[0], meta[1]
    span = pl.ds(pl.multiple_of(feat * QR, QR), QR)
    copy = pltpu.make_async_copy(heavy.at[:, span, :], quarter.at[pl.ds(0, NH)], sem)
    copy.start()
    quarter[NH] = jnp.zeros((QR, T), BF16)

    def clear(q, carry):
        taken[q] = 0
        seats[2 * q] = NH
        seats[2 * q + 1] = NH
        return carry

    lax.fori_loop(0, NG, clear, 0, unroll=8)

    def seat(i, carry):
        q = slots[0, i // HT, i % HT]
        turn = taken[q]
        taken[q] = turn + 1
        seats[2 * q + turn] = i
        return carry

    lax.fori_loop(0, NH, seat, 0, unroll=8)
    lane = lax.broadcasted_iota(jnp.int32, (NOTES, T), 1)
    copy.wait()

    def node(i):
        j = jnp.minimum(i, NH - 1)
        tile = ((blk - (j >> 3)) & (NB - 1)) * 2 * NR + cols[0, j >> 3, j & (HT - 1)]
        return jnp.where(i < NH, tile, NT)

    def fill(q, carry):
        a, b = seats[2 * q], seats[2 * q + 1]
        notes = jnp.where(lane == 0, node(a), node(b)).astype(jnp.float32).astype(BF16)
        out[q] = jnp.concatenate([quarter[a], quarter[b], notes], axis=0)
        return carry

    lax.fori_loop(0, NG, fill, 0, unroll=4)

    for g in range(FAR_AT // STEP):
        need[g] = 0

    def put(k, carry, s, start, j, base):
        n0, n1 = carry
        row, col = rows[0, s, k], lcols[0, s, k]
        at = base + jnp.where(row == 0, n0, n1)
        ids[row, at] = j * LT + k
        places[row, at] = start + (col & 1) * NG + (col >> 1)
        if base == 0:
            need[at >> 4] = j
        return n0 + 1 - row, n1 + row

    def pad(i, carry, t):
        ids[t, i] = 0
        places[t, i] = NT
        return carry

    for which, (base, blocks) in enumerate(((0, range(NEAR_STEPS)), (FAR_AT, range(NEAR_STEPS, NB)))):
        counts = (0, 0)
        for j in blocks:
            s, start = step_of(blk, j)
            counts = lax.fori_loop(
                0, LT, lambda k, c, s=s, v=start, j=j, b=base: put(k, c, s, v, j, b), counts, unroll=6
            )
        count = (jnp.maximum(counts[0], counts[1]) + STEP - 1) // STEP
        trips[which] = count
        for t in range(2):
            lax.fori_loop(base + counts[t], base + count * STEP, lambda i, c, t=t: pad(i, c, t), 0)


def compact_kernel(hplaces, ids, places, htrips):
    def clear(i, carry):
        ids[i] = 0
        places[i] = NT
        return carry

    lax.fori_loop(0, NL, clear, 0, unroll=8)

    def put(i, n):
        place = hplaces[i]
        ids[n] = i
        places[n] = place
        return n + jnp.where(place < NT, 1, 0)

    n = lax.fori_loop(0, SLOTS, put, 0, unroll=8)
    ids[n] = 0
    places[n] = NT
    htrips[0] = (n + STEP - 1) // STEP


def dots(tile, value, count, ids, places, acc):
    for u in range(0, count, 2):
        left = jnp.concatenate([tile(ids(u)), tile(ids(u + 1))], axis=1)
        right = jnp.concatenate([value(places(u)), value(places(u + 1))], axis=0)
        acc = acc + jnp.dot(left, right, preferred_element_type=jnp.float32)
    return acc


def light_copy(meta, light, tiles, j, first, rows, sem):
    step, _ = step_of(meta[0], j)
    source = light.at[pl.ds(step * LT, LT)]
    if rows is not None:
        source = light.at[pl.ds(step * LT, LT), rows, :]
    return pltpu.make_async_copy(source, tiles.at[pl.ds((j - first) * LT, LT)], sem)


def light_dots(tiles, value, ids, places, first, base, carry):
    return [
        dots(
            lambda i: tiles[jnp.maximum(i - first * LT, 0)], value, STEP,
            lambda u: ids[t, base + u], lambda u: places[t, base + u], carry[t],
        )
        for t in range(2)
    ]


def feature_copies(meta, held, parts, values, sems):
    core = meta[2]
    copies = []
    for which in range(2):
        c = core if which == 0 else 1 - core
        for (start, size), part in zip(held, parts[which * len(held) : (which + 1) * len(held)]):
            span = pl.ds(c * NG + start, size)
            copies.append(pltpu.make_async_copy(part, values.at[span], sems.at[len(copies)]))
    return copies


def first_near_kernel(meta, trips, ids, places, light, *rest):
    held = HELD[:3]
    parts, (out, values, tiles, sems) = rest[: 2 * len(held)], rest[2 * len(held) :]
    rows = pl.ds(pl.multiple_of(meta[1] * QR, QR), QR)
    copies = feature_copies(meta, held, parts, values, sems)
    for j in range(NEAR_STEPS):
        copies.append(light_copy(meta, light, tiles, j, 0, rows, sems.at[len(copies)]))
    for copy in copies:
        copy.start()
    values[NT] = jnp.zeros((T, T), BF16)
    for copy in copies:
        copy.wait()
    zero = jnp.zeros((QR, T), jnp.float32)
    body = lambda g, c: light_dots(tiles, lambda p: values[p], ids, places, 0, g * STEP, c)
    out[0], out[1] = lax.fori_loop(0, trips[0], body, [zero, zero])


def first_kernel(meta, trips, ids, places, hplaces, light, heavy, near, *rest):
    parts, (out, values, tiles, htiles, sems) = rest[: 2 * len(HELD)], rest[2 * len(HELD) :]
    owner = meta[3]
    rows = pl.ds(pl.multiple_of(meta[1] * QR, QR), QR)
    copies = feature_copies(meta, HELD, parts, values, sems)
    for j in range(NEAR_STEPS, NB):
        copies.append(light_copy(meta, light, tiles, j, NEAR_STEPS, rows, sems.at[len(copies)]))
    for slot in range(2):
        rows, span = pl.ds(slot * QR, QR), pl.ds(slot * NG, NG)
        copies.append(
            pltpu.make_async_copy(heavy.at[:, rows, :], htiles.at[span], sems.at[len(copies)])
        )
    for copy in copies:
        copy.start()
    values[NT] = jnp.zeros((T, T), BF16)
    for copy in copies:
        copy.wait()
    value = lambda p: values[p]
    body = lambda g, c: light_dots(tiles, value, ids, places, NEAR_STEPS, FAR_AT + g * STEP, c)
    sums = lax.fori_loop(0, trips[1], body, [near[0], near[1]])

    def heavy_body(g, acc):
        base = g * HSTEP
        return dots(
            lambda i: htiles[i], value, HSTEP,
            lambda u: base + u, lambda u: hplaces[base + u], acc,
        )

    hsum = lax.fori_loop(0, SLOTS // HSTEP, heavy_body, jnp.zeros((QR, T), jnp.float32))
    for t in range(2):
        total = (sums[t] + jnp.where(owner == t, hsum, 0.0)).astype(BF16)
        for n in range(2 * NPLANE):
            out[n, t] = total


def project_kernel(n, *refs):
    parts, (w_in, b_in, w_mid, mine, theirs) = refs[:n], refs[n:]
    at = 0
    for part in parts:
        size = part.shape[0]
        for rt in range(2):
            x = part[:, :, rt].reshape(-1, T)
            h = jnp.dot(x, w_in[...], preferred_element_type=jnp.float32) + b_in[...]
            h = jnp.maximum(h, 0.0).astype(BF16)
            s = jnp.dot(h, w_mid[...], preferred_element_type=jnp.float32).astype(BF16)
            mine[rt, at : at + size] = s[:, :T].reshape(size, *mine.shape[2:])
            theirs[rt, at : at + size] = s[:, T:].reshape(size, *mine.shape[2:])
        at += size


def value_copies(meta, held, parts, values, sems):
    copies = []
    for which in range(2):
        c = meta[2] if which == 0 else 1 - meta[2]
        for k, at, start, size in held:
            part = parts[which * (held[-1][0] + 1) + k]
            for rt in range(2):
                span = pl.ds(rt * NG + start, size)
                copies.append(
                    pltpu.make_async_copy(
                        part.at[rt, pl.ds(at, size)], values.at[span, :, c], sems.at[len(copies)]
                    )
                )
    return copies


def second_near_kernel(meta, trips, need, ids, places, light, *rest):
    parts, (out, values, tiles, sems, light_sems) = rest[:4], rest[4:]
    copies = value_copies(meta, PROJECTED[:3], parts, values, sems)
    chunks = [light_copy(meta, light, tiles, j, 0, None, light_sems.at[j]) for j in range(NEAR_STEPS)]
    for copy in copies + chunks:
        copy.start()
    values[NT] = jnp.zeros((2, 2, QR, T), BF16)
    for copy in copies:
        copy.wait()

    def wait_for(n):
        span = pl.ds(n * LT, LT)
        pltpu.make_async_copy(light.at[span], tiles.at[span], light_sems.at[n]).wait()
        return n + 1

    value = lambda p: values[p].reshape(T, T)

    def body(g, carry):
        here = lax.while_loop(lambda n: n <= need[g], wait_for, carry[2])
        return (*light_dots(tiles, value, ids, places, 0, g * STEP, carry[:2]), here)

    zero = jnp.zeros((T, T), jnp.float32)
    sum0, sum1, here = lax.fori_loop(0, trips[0], body, (zero, zero, 0))
    lax.while_loop(lambda n: n < NEAR_STEPS, wait_for, here)
    out[0] = sum0
    out[1] = sum1


def second_kernel(
    meta, trips, htrips, ids, places, hids, hplaces, light, h0, h1, h2, h3, near, b_mid, *rest
):
    parts, (out, values, tiles, htiles, sems) = rest[:6], rest[6:]
    feat, owner = meta[1], meta[3]
    copies = value_copies(meta, PROJECTED, parts, values, sems)
    for j in range(NEAR_STEPS, NB):
        copies.append(light_copy(meta, light, tiles, j, NEAR_STEPS, None, sems.at[len(copies)]))
    first = len(copies)
    for k, h in enumerate((h0, h1, h2, h3)):
        rows = pl.ds(pl.multiple_of((feat ^ k) * QR, QR), QR)
        for slot in range(2):
            copies.append(
                pltpu.make_async_copy(
                    h.at[:, pl.ds(slot * QR, QR), :],
                    htiles.at[pl.ds(slot * NG, NG), rows, :],
                    sems.at[len(copies)],
                )
            )
    for copy in copies:
        copy.start()
    values[NT] = jnp.zeros((2, 2, QR, T), BF16)
    for copy in copies[:first]:
        copy.wait()
    value = lambda p: values[p].reshape(T, T)
    body = lambda g, c: light_dots(tiles, value, ids, places, NEAR_STEPS, FAR_AT + g * STEP, c)
    sums = lax.fori_loop(0, trips[1], body, [near[0], near[1]])
    for copy in copies[first:]:
        copy.wait()

    def heavy_body(g, acc):
        base = g * STEP
        return dots(
            lambda i: htiles[i], value, STEP, lambda u: hids[base + u], lambda u: hplaces[base + u], acc
        )

    hsum = lax.fori_loop(0, htrips[0], heavy_body, jnp.zeros((T, T), jnp.float32))
    for t in range(2):
        total = sums[t] + jnp.where(owner == t, hsum, 0.0) + b_mid[...]
        out[t * T : (t + 1) * T] = total.astype(BF16)


def per_device(
    features, weight_in, bias_in, weight_mid, bias_mid, light_tiles, light_rows, light_cols,
    heavy_tiles, heavy_slots, heavy_cols, owner_map,
):
    i32 = jnp.int32
    blk, core, feat = lax.axis_index(BLK), lax.axis_index("c"), lax.axis_index(FEAT)
    meta = jnp.stack([blk, feat, core, owner_map[0]]).astype(i32)
    light = light_tiles.reshape(NL, T, T)
    int_list = jax.ShapeDtypeStruct((NL,), i32)
    int_lists = jax.ShapeDtypeStruct((2, LIST), i32)
    needs = jax.ShapeDtypeStruct((FAR_AT // STEP,), i32)
    one_int = jax.ShapeDtypeStruct((1,), i32)
    two_ints = jax.ShapeDtypeStruct((2,), i32)

    half = lax.dynamic_slice_in_dim(features, core * T, T, axis=0)
    plane = everyone(half, PLANE, NPLANE)

    packed, ids, places, need, trips = pl.pallas_call(
        pack_kernel,
        out_shape=(
            jax.ShapeDtypeStruct((NG, 2 * QR + NOTES, T), BF16), int_lists, int_lists, needs, two_ints
        ),
        in_specs=[SMEM] * 5 + [ANY],
        out_specs=(VMEM, SMEM, SMEM, SMEM, SMEM),
        scratch_shapes=[
            pltpu.VMEM((NH + 1, QR, T), BF16),
            pltpu.SMEM((SLOTS,), i32),
            pltpu.SMEM((NG,), i32),
            pltpu.SemaphoreType.DMA(()),
        ],
        compiler_params=params(16),
        cost_estimate=pl.CostEstimate(flops=0, transcendentals=0, bytes_accessed=30_000_000),
        name="pack",
    )(meta, heavy_slots, heavy_cols, light_rows, light_cols, heavy_tiles.reshape(NH, T, T))
    arrived = lax.all_to_all(packed, GROUP, 0, 0, tiled=True)
    own = along_x(plane)
    own, far_parts = own[:3], own[3:]
    other = [swap(part, "c") for part in own]

    nodes = arrived[:, 2 * QR, :2].T.reshape(SLOTS).astype(i32)
    hplaces = jnp.where(
        nodes < NT, (nodes & 1) * NG + turned(blk, nodes >> 4) * NR + ((nodes & 15) >> 1), NT
    )

    first_near = pl.pallas_call(
        first_near_kernel,
        out_shape=jax.ShapeDtypeStruct((2, QR, T), jnp.float32),
        in_specs=[SMEM] * 4 + [ANY] * 7,
        out_specs=VMEM,
        scratch_shapes=[
            pltpu.VMEM((NT + 1, T, T), BF16),
            pltpu.VMEM((NEAR_STEPS * LT, QR, T), BF16),
            pltpu.SemaphoreType.DMA((6 + NEAR_STEPS,)),
        ],
        compiler_params=params(54),
        name="first_near",
    )(meta, trips, ids, places, light, *own, *other)
    first_near, far_parts = lax.optimization_barrier((first_near, far_parts))
    held = own + far_parts + other + [swap(part, "c") for part in far_parts]
    aggregated = pl.pallas_call(
        first_kernel,
        out_shape=jax.ShapeDtypeStruct((2 * NPLANE, 2, QR, T), BF16),
        in_specs=[SMEM] * 5 + [ANY] * 2 + [VMEM] + [ANY] * len(held),
        out_specs=VMEM,
        scratch_shapes=[
            pltpu.VMEM((NT + 1, T, T), BF16),
            pltpu.VMEM(((NB - NEAR_STEPS) * LT, QR, T), BF16),
            pltpu.VMEM((SLOTS, QR, T), BF16),
            pltpu.SemaphoreType.DMA((len(held) + 4,)),
        ],
        compiler_params=params(54),
        name="first",
    )(meta, trips, ids, places, hplaces, light, arrived, first_near, *held)

    aggregated, weight_in, bias_in, weight_mid = lax.optimization_barrier(
        (aggregated, weight_in, bias_in, weight_mid)
    )
    bias_rows = jnp.pad(bias_in.reshape(1, T), ((0, 7), (0, 0)))
    pieces = jnp.concatenate([weight_in.astype(jnp.float32), bias_rows], axis=0)
    pieces = jnp.stack([pieces, swap(pieces, "yl")])
    pieces = jnp.stack([pieces, swap(pieces, "c")], axis=1).reshape(4, T + 8, T)
    pieces = jnp.take(pieces, feat ^ jnp.arange(4), axis=0)
    w_in = jnp.moveaxis(pieces[:, :T], 0, 1).reshape(T, 4 * T).astype(BF16)
    b_in = pieces[:, T].reshape(1, 4 * T)
    w_mid = jnp.concatenate([weight_mid, swap(weight_mid, "c")], axis=1)

    rows = lax.all_to_all(aggregated, (*PLANE, "yl"), 0, 0, tiled=True).reshape(NPLANE, 2, 2, QR, T)

    hids, hlist, htrips = pl.pallas_call(
        compact_kernel,
        out_shape=(int_list, int_list, one_int),
        in_specs=[SMEM],
        out_specs=(SMEM,) * 3,
        name="compact",
    )(hplaces)

    rows, arrived, w_in, b_in, w_mid, hids, hlist, htrips = lax.optimization_barrier(
        (rows, arrived, w_in, b_in, w_mid, hids, hlist, htrips)
    )
    hc = swap(arrived, "c")
    hy = swap(arrived, "yl")
    def project(*parts):
        groups = sum(part.shape[0] for part in parts)
        half_values = jax.ShapeDtypeStruct((2, groups, 2, QR, T), BF16)
        return pl.pallas_call(
            functools.partial(project_kernel, len(parts)),
            out_shape=(half_values, half_values),
            in_specs=[VMEM] * (len(parts) + 3),
            out_specs=(VMEM, VMEM),
            compiler_params=params(24),
            name="project",
        )(*parts, w_in, b_in, w_mid)

    behind = lax.ppermute(rows, "x", around("x", 1))
    ahead = lax.ppermute(rows, "x", around("x", -1))
    near = project(rows)
    behind, ahead, near = lax.optimization_barrier((behind, ahead, near))
    far = [
        lax.ppermute(behind[:NR], "x", around("x", 1)),
        lax.ppermute(ahead[NR:], "x", around("x", -1)),
    ]
    sides = project(behind, ahead)
    mine = [near[0], sides[0]]
    swapped = [swap(near[1], "c"), swap(sides[1], "c")]
    second_near = pl.pallas_call(
        second_near_kernel,
        out_shape=jax.ShapeDtypeStruct((2, T, T), jnp.float32),
        in_specs=[SMEM] * 5 + [ANY] * 5,
        out_specs=VMEM,
        scratch_shapes=[
            pltpu.VMEM((NT + 1, 2, 2, QR, T), BF16),
            pltpu.VMEM((NEAR_STEPS * LT, T, T), BF16),
            pltpu.SemaphoreType.DMA((12,)),
            pltpu.SemaphoreType.DMA((NEAR_STEPS,)),
        ],
        compiler_params=params(54),
        name="second_near",
    )(meta, trips, need, ids, places, light, *mine, *swapped)
    far, second_near = lax.optimization_barrier((far, second_near))
    far = project(*far)
    mine.append(far[0])
    swapped.append(swap(far[1], "c"))
    hy_late, _ = lax.optimization_barrier((hy, far))
    hyc = swap(hy_late, "c")
    return pl.pallas_call(
        second_kernel,
        out_shape=jax.ShapeDtypeStruct((2 * T, T), BF16),
        in_specs=[SMEM] * 7 + [ANY] * 5 + [VMEM] * 2 + [ANY] * 6,
        out_specs=VMEM,
        scratch_shapes=[
            pltpu.VMEM((NT + 1, 2, 2, QR, T), BF16),
            pltpu.VMEM(((NB - NEAR_STEPS) * LT, T, T), BF16),
            pltpu.VMEM((SLOTS, T, T), BF16),
            pltpu.SemaphoreType.DMA((26,)),
        ],
        compiler_params=params(54),
        name="second",
    )(
        meta, trips, htrips, ids, places, hids, hlist, light, arrived, hc, hy, hyc, second_near,
        bias_mid.reshape(1, T), *mine, *swapped,
    )


def solution(mesh):
    wide = Mesh(mesh.devices.reshape(4, 2, 8, 2, 2), ("x", "yh", "z", "yl", "c"))
    in_specs = (
        P(GROUP, None),
        P(None, FEAT),
        P(FEAT),
        P(None, FEAT),
        P(FEAT),
        P(GROUP, None, None, None, None),
        P(GROUP, None, None),
        P(GROUP, None, None),
        P(GROUP, None, None, None, None),
        P(GROUP, None, None),
        P(GROUP, None, None),
        P(GROUP),
    )
    return jax.shard_map(
        per_device, mesh=wide, in_specs=in_specs, out_specs=P(GROUP, FEAT), check_vma=False
    )
```

```python
import functools

import jax
import jax.numpy as jnp
from jax import lax
from jax.experimental import pallas as pl
from jax.experimental.pallas import tpu as pltpu
from jax.sharding import Mesh
from jax.sharding import PartitionSpec as P

BLK = ("x", "yh")
GROUP = ("x", "yh", "z")
FEAT = ("yl", "c")
PLANE = ("yh", "z")
T = 128
NB = 8
NR = 8
NG = NB * NR
NT = 2 * NG
LT = 36
HT = 8
NL = NB * LT
NH = NB * HT
SLOTS = 2 * NG
QR = T // 4
STEP = 16
NOTES = 8
NX = 4
NPLANE = 2 * NR
HSTEP = 32
NEAR_STEPS = NB - 2
FAR_AT = -(-NEAR_STEPS * LT // STEP) * STEP
LIST = FAR_AT + -(-2 * LT // STEP) * STEP
HELD = ((0, NPLANE), (NPLANE, NPLANE), (3 * NPLANE, NPLANE), (2 * NPLANE, NR), (2 * NPLANE + NR, NR))
BF16 = jnp.bfloat16
SMEM = pl.BlockSpec(memory_space=pltpu.SMEM)
VMEM = pl.BlockSpec(memory_space=pltpu.VMEM)
ANY = pl.BlockSpec(memory_space=pl.ANY)
HBM = pl.BlockSpec(memory_space=pltpu.MemorySpace.HBM)


def params(mib):
    return pltpu.CompilerParams(vmem_limit_bytes=mib * 1024 * 1024)


def turned(blk, source):
    return (((blk >> 1) - (source >> 1)) & 3) * 2 + (source & 1)

PROJECTED = ((0, 0, 0, NPLANE), (1, 0, NPLANE, NPLANE), (1, NPLANE, 3 * NPLANE, NPLANE), (2, 0, 2 * NPLANE, NPLANE))


def step_of(blk, j):
    order = j if j < 4 else (j + 2 if j < NEAR_STEPS else j - 2)
    held, y = order >> 1, order & 1
    source = (((blk >> 1) - held) & 3) * 2 + y
    return (blk - source) & (NB - 1), order * NR


def around(axis, distance):
    n = lax.axis_size(axis)
    return [(i, (i + distance) % n) for i in range(n)]


def along_x(near):
    behind = lax.ppermute(near, "x", around("x", 1))
    ahead = lax.ppermute(near, "x", around("x", -1))
    far = near.shape[0] // 2
    return [
        near,
        behind,
        ahead,
        lax.ppermute(behind[:far], "x", around("x", 1)),
        lax.ppermute(ahead[far:], "x", around("x", -1)),
    ]


def swap(x, axis):
    return lax.ppermute(x, axis, around(axis, 1))


def everyone(x, axis, n):
    spread = jnp.broadcast_to(x[None], (n, *x.shape))
    return lax.all_to_all(spread, axis, 0, 0, tiled=True)


def pack_kernel(
    meta, slots, cols, rows, lcols, heavy, out, ids, places, need, trips, quarter, seats, taken, sem
):
    blk, feat = meta[0], meta[1]
    span = pl.ds(pl.multiple_of(feat * QR, QR), QR)
    copy = pltpu.make_async_copy(heavy.at[:, span, :], quarter.at[pl.ds(0, NH)], sem)
    copy.start()
    quarter[NH] = jnp.zeros((QR, T), BF16)

    def clear(q, carry):
        taken[q] = 0
        seats[2 * q] = NH
        seats[2 * q + 1] = NH
        return carry

    lax.fori_loop(0, NG, clear, 0, unroll=8)

    def seat(i, carry):
        q = slots[0, i // HT, i % HT]
        turn = taken[q]
        taken[q] = turn + 1
        seats[2 * q + turn] = i
        return carry

    lax.fori_loop(0, NH, seat, 0, unroll=8)
    lane = lax.broadcasted_iota(jnp.int32, (NOTES, T), 1)
    copy.wait()

    def node(i):
        j = jnp.minimum(i, NH - 1)
        tile = ((blk - (j >> 3)) & (NB - 1)) * 2 * NR + cols[0, j >> 3, j & (HT - 1)]
        return jnp.where(i < NH, tile, NT)

    def fill(q, carry):
        a, b = seats[2 * q], seats[2 * q + 1]
        notes = jnp.where(lane == 0, node(a), node(b)).astype(jnp.float32).astype(BF16)
        out[q] = jnp.concatenate([quarter[a], quarter[b], notes], axis=0)
        return carry

    lax.fori_loop(0, NG, fill, 0, unroll=4)

    for g in range(FAR_AT // STEP):
        need[g] = 0

    def put(k, carry, s, start, j, base):
        n0, n1 = carry
        row, col = rows[0, s, k], lcols[0, s, k]
        at = base + jnp.where(row == 0, n0, n1)
        ids[row, at] = j * LT + k
        places[row, at] = start + (col & 1) * NG + (col >> 1)
        if base == 0:
            need[at >> 4] = j
        return n0 + 1 - row, n1 + row

    def pad(i, carry, t):
        ids[t, i] = 0
        places[t, i] = NT
        return carry

    for which, (base, blocks) in enumerate(((0, range(NEAR_STEPS)), (FAR_AT, range(NEAR_STEPS, NB)))):
        counts = (0, 0)
        for j in blocks:
            s, start = step_of(blk, j)
            counts = lax.fori_loop(
                0, LT, lambda k, c, s=s, v=start, j=j, b=base: put(k, c, s, v, j, b), counts, unroll=6
            )
        count = (jnp.maximum(counts[0], counts[1]) + STEP - 1) // STEP
        trips[which] = count
        for t in range(2):
            lax.fori_loop(base + counts[t], base + count * STEP, lambda i, c, t=t: pad(i, c, t), 0)


def compact_kernel(hplaces, ids, places, htrips):
    def clear(i, carry):
        ids[i] = 0
        places[i] = NT
        return carry

    lax.fori_loop(0, NL, clear, 0, unroll=8)

    def put(i, n):
        place = hplaces[i]
        ids[n] = i
        places[n] = place
        return n + jnp.where(place < NT, 1, 0)

    n = lax.fori_loop(0, SLOTS, put, 0, unroll=8)
    ids[n] = 0
    places[n] = NT
    htrips[0] = (n + STEP - 1) // STEP


def dots(tile, value, count, ids, places, acc):
    for u in range(0, count, 2):
        left = jnp.concatenate([tile(ids(u)), tile(ids(u + 1))], axis=1)
        right = jnp.concatenate([value(places(u)), value(places(u + 1))], axis=0)
        acc = acc + jnp.dot(left, right, preferred_element_type=jnp.float32)
    return acc


def light_copy(meta, light, tiles, j, first, rows, sem):
    step, _ = step_of(meta[0], j)
    source = light.at[pl.ds(step * LT, LT)]
    if rows is not None:
        source = light.at[pl.ds(step * LT, LT), rows, :]
    return pltpu.make_async_copy(source, tiles.at[pl.ds((j - first) * LT, LT)], sem)


def light_dots(tiles, value, ids, places, first, base, carry):
    return [
        dots(
            lambda i: tiles[jnp.maximum(i - first * LT, 0)], value, STEP,
            lambda u: ids[t, base + u], lambda u: places[t, base + u], carry[t],
        )
        for t in range(2)
    ]


def feature_copies(meta, held, parts, values, sems):
    core = meta[2]
    copies = []
    for which in range(2):
        c = core if which == 0 else 1 - core
        for (start, size), part in zip(held, parts[which * len(held) : (which + 1) * len(held)]):
            span = pl.ds(c * NG + start, size)
            copies.append(pltpu.make_async_copy(part, values.at[span], sems.at[len(copies)]))
    return copies


def first_near_kernel(meta, trips, ids, places, light, *rest):
    held = HELD[:3]
    parts, (out, values, tiles, sems) = rest[: 2 * len(held)], rest[2 * len(held) :]
    rows = pl.ds(pl.multiple_of(meta[1] * QR, QR), QR)
    copies = feature_copies(meta, held, parts, values, sems)
    for j in range(NEAR_STEPS):
        copies.append(light_copy(meta, light, tiles, j, 0, rows, sems.at[len(copies)]))
    for copy in copies:
        copy.start()
    values[NT] = jnp.zeros((T, T), BF16)
    for copy in copies:
        copy.wait()
    zero = jnp.zeros((QR, T), jnp.float32)
    body = lambda g, c: light_dots(tiles, lambda p: values[p], ids, places, 0, g * STEP, c)
    out[0], out[1] = lax.fori_loop(0, trips[0], body, [zero, zero])


def first_kernel(meta, trips, ids, places, hplaces, light, heavy, near, *rest):
    parts, (out, values, tiles, htiles, sems) = rest[: 2 * len(HELD)], rest[2 * len(HELD) :]
    owner = meta[3]
    rows = pl.ds(pl.multiple_of(meta[1] * QR, QR), QR)
    copies = feature_copies(meta, HELD, parts, values, sems)
    for j in range(NEAR_STEPS, NB):
        copies.append(light_copy(meta, light, tiles, j, NEAR_STEPS, rows, sems.at[len(copies)]))
    for slot in range(2):
        rows, span = pl.ds(slot * QR, QR), pl.ds(slot * NG, NG)
        copies.append(
            pltpu.make_async_copy(heavy.at[:, rows, :], htiles.at[span], sems.at[len(copies)])
        )
    for copy in copies:
        copy.start()
    values[NT] = jnp.zeros((T, T), BF16)
    for copy in copies:
        copy.wait()
    value = lambda p: values[p]
    body = lambda g, c: light_dots(tiles, value, ids, places, NEAR_STEPS, FAR_AT + g * STEP, c)
    sums = lax.fori_loop(0, trips[1], body, [near[0], near[1]])

    def heavy_body(g, acc):
        base = g * HSTEP
        return dots(
            lambda i: htiles[i], value, HSTEP,
            lambda u: base + u, lambda u: hplaces[base + u], acc,
        )

    hsum = lax.fori_loop(0, SLOTS // HSTEP, heavy_body, jnp.zeros((QR, T), jnp.float32))
    for t in range(2):
        total = (sums[t] + jnp.where(owner == t, hsum, 0.0)).astype(BF16)
        for n in range(2 * NPLANE):
            out[n, t] = total


def project_kernel(n, *refs):
    parts, (w_in, b_in, w_mid, mine, theirs) = refs[:n], refs[n:]
    at = 0
    for part in parts:
        size = part.shape[0]
        for rt in range(2):
            x = part[:, :, rt].reshape(-1, T)
            h = jnp.dot(x, w_in[...], preferred_element_type=jnp.float32) + b_in[...]
            h = jnp.maximum(h, 0.0).astype(BF16)
            s = jnp.dot(h, w_mid[...], preferred_element_type=jnp.float32).astype(BF16)
            mine[rt, at : at + size] = s[:, :T].reshape(size, *mine.shape[2:])
            theirs[rt, at : at + size] = s[:, T:].reshape(size, *mine.shape[2:])
        at += size


def value_copies(meta, held, parts, values, sems):
    copies = []
    for which in range(2):
        c = meta[2] if which == 0 else 1 - meta[2]
        for k, at, start, size in held:
            part = parts[which * (held[-1][0] + 1) + k]
            for rt in range(2):
                span = pl.ds(rt * NG + start, size)
                copies.append(
                    pltpu.make_async_copy(
                        part.at[rt, pl.ds(at, size)], values.at[span, :, c], sems.at[len(copies)]
                    )
                )
    return copies


def second_near_kernel(meta, trips, need, ids, places, light, *rest):
    parts, (out, values, tiles, sems, light_sems) = rest[:4], rest[4:]
    copies = value_copies(meta, PROJECTED[:3], parts, values, sems)
    chunks = [light_copy(meta, light, tiles, j, 0, None, light_sems.at[j]) for j in range(NEAR_STEPS)]
    for copy in copies + chunks:
        copy.start()
    values[NT] = jnp.zeros((2, 2, QR, T), BF16)
    for copy in copies:
        copy.wait()

    def wait_for(n):
        span = pl.ds(n * LT, LT)
        pltpu.make_async_copy(light.at[span], tiles.at[span], light_sems.at[n]).wait()
        return n + 1

    value = lambda p: values[p].reshape(T, T)

    def body(g, carry):
        here = lax.while_loop(lambda n: n <= need[g], wait_for, carry[2])
        return (*light_dots(tiles, value, ids, places, 0, g * STEP, carry[:2]), here)

    zero = jnp.zeros((T, T), jnp.float32)
    sum0, sum1, here = lax.fori_loop(0, trips[0], body, (zero, zero, 0))
    lax.while_loop(lambda n: n < NEAR_STEPS, wait_for, here)
    out[0] = sum0
    out[1] = sum1


def second_kernel(
    meta, trips, htrips, ids, places, hids, hplaces, light, h0, h1, h2, h3, near, b_mid, *rest
):
    parts, (out, values, tiles, htiles, sems) = rest[:6], rest[6:]
    feat, owner = meta[1], meta[3]
    copies = value_copies(meta, PROJECTED, parts, values, sems)
    for j in range(NEAR_STEPS, NB):
        copies.append(light_copy(meta, light, tiles, j, NEAR_STEPS, None, sems.at[len(copies)]))
    first = len(copies)
    for k, h in enumerate((h0, h1, h2, h3)):
        rows = pl.ds(pl.multiple_of((feat ^ k) * QR, QR), QR)
        for slot in range(2):
            copies.append(
                pltpu.make_async_copy(
                    h.at[:, pl.ds(slot * QR, QR), :],
                    htiles.at[pl.ds(slot * NG, NG), rows, :],
                    sems.at[len(copies)],
                )
            )
    for copy in copies:
        copy.start()
    values[NT] = jnp.zeros((2, 2, QR, T), BF16)
    for copy in copies[:first]:
        copy.wait()
    value = lambda p: values[p].reshape(T, T)
    body = lambda g, c: light_dots(tiles, value, ids, places, NEAR_STEPS, FAR_AT + g * STEP, c)
    sums = lax.fori_loop(0, trips[1], body, [near[0], near[1]])
    for copy in copies[first:]:
        copy.wait()

    def heavy_body(g, acc):
        base = g * STEP
        return dots(
            lambda i: htiles[i], value, STEP, lambda u: hids[base + u], lambda u: hplaces[base + u], acc
        )

    hsum = lax.fori_loop(0, htrips[0], heavy_body, jnp.zeros((T, T), jnp.float32))
    for t in range(2):
        total = sums[t] + jnp.where(owner == t, hsum, 0.0) + b_mid[...]
        out[t * T : (t + 1) * T] = total.astype(BF16)


def per_device(
    features, weight_in, bias_in, weight_mid, bias_mid, light_tiles, light_rows, light_cols,
    heavy_tiles, heavy_slots, heavy_cols, owner_map,
):
    i32 = jnp.int32
    blk, core, feat = lax.axis_index(BLK), lax.axis_index("c"), lax.axis_index(FEAT)
    meta = jnp.stack([blk, feat, core, owner_map[0]]).astype(i32)
    in_hbm = lambda x: pltpu.with_memory_space_constraint(x, pltpu.MemorySpace.HBM)
    light = in_hbm(light_tiles.reshape(NL, T, T))
    int_list = jax.ShapeDtypeStruct((NL,), i32)
    int_lists = jax.ShapeDtypeStruct((2, LIST), i32)
    needs = jax.ShapeDtypeStruct((FAR_AT // STEP,), i32)
    one_int = jax.ShapeDtypeStruct((1,), i32)
    two_ints = jax.ShapeDtypeStruct((2,), i32)

    half = lax.dynamic_slice_in_dim(features, core * T, T, axis=0)
    plane = everyone(half, PLANE, NPLANE)

    packed, ids, places, need, trips = pl.pallas_call(
        pack_kernel,
        out_shape=(
            jax.ShapeDtypeStruct((NG, 2 * QR + NOTES, T), BF16), int_lists, int_lists, needs, two_ints
        ),
        in_specs=[SMEM] * 5 + [HBM],
        out_specs=(VMEM, SMEM, SMEM, SMEM, SMEM),
        scratch_shapes=[
            pltpu.VMEM((NH + 1, QR, T), BF16),
            pltpu.SMEM((SLOTS,), i32),
            pltpu.SMEM((NG,), i32),
            pltpu.SemaphoreType.DMA(()),
        ],
        compiler_params=params(16),
        cost_estimate=pl.CostEstimate(flops=0, transcendentals=0, bytes_accessed=30_000_000),
        name="pack",
    )(meta, heavy_slots, heavy_cols, light_rows, light_cols, in_hbm(heavy_tiles.reshape(NH, T, T)))
    arrived = lax.all_to_all(packed, GROUP, 0, 0, tiled=True)
    own = along_x(plane)
    own, far_parts = own[:3], own[3:]
    other = [swap(part, "c") for part in own]

    nodes = arrived[:, 2 * QR, :2].T.reshape(SLOTS).astype(i32)
    hplaces = jnp.where(
        nodes < NT, (nodes & 1) * NG + turned(blk, nodes >> 4) * NR + ((nodes & 15) >> 1), NT
    )

    first_near = pl.pallas_call(
        first_near_kernel,
        out_shape=jax.ShapeDtypeStruct((2, QR, T), jnp.float32),
        in_specs=[SMEM] * 4 + [HBM] + [ANY] * 6,
        out_specs=VMEM,
        scratch_shapes=[
            pltpu.VMEM((NT + 1, T, T), BF16),
            pltpu.VMEM((NEAR_STEPS * LT, QR, T), BF16),
            pltpu.SemaphoreType.DMA((6 + NEAR_STEPS,)),
        ],
        compiler_params=params(24),
        name="first_near",
    )(meta, trips, ids, places, light, *own, *other)
    first_near, far_parts = lax.optimization_barrier((first_near, far_parts))
    held = own + far_parts + other + [swap(part, "c") for part in far_parts]
    aggregated = pl.pallas_call(
        first_kernel,
        out_shape=jax.ShapeDtypeStruct((2 * NPLANE, 2, QR, T), BF16),
        in_specs=[SMEM] * 5 + [HBM, ANY, VMEM] + [ANY] * len(held),
        out_specs=VMEM,
        scratch_shapes=[
            pltpu.VMEM((NT + 1, T, T), BF16),
            pltpu.VMEM(((NB - NEAR_STEPS) * LT, QR, T), BF16),
            pltpu.VMEM((SLOTS, QR, T), BF16),
            pltpu.SemaphoreType.DMA((len(held) + 4,)),
        ],
        compiler_params=params(24),
        name="first",
    )(meta, trips, ids, places, hplaces, light, arrived, first_near, *held)

    aggregated, weight_in, bias_in, weight_mid = lax.optimization_barrier(
        (aggregated, weight_in, bias_in, weight_mid)
    )
    bias_rows = jnp.pad(bias_in.reshape(1, T), ((0, 7), (0, 0)))
    pieces = jnp.concatenate([weight_in.astype(jnp.float32), bias_rows], axis=0)
    pieces = jnp.stack([pieces, swap(pieces, "yl")])
    pieces = jnp.stack([pieces, swap(pieces, "c")], axis=1).reshape(4, T + 8, T)
    pieces = jnp.take(pieces, feat ^ jnp.arange(4), axis=0)
    w_in = jnp.moveaxis(pieces[:, :T], 0, 1).reshape(T, 4 * T).astype(BF16)
    b_in = pieces[:, T].reshape(1, 4 * T)
    w_mid = jnp.concatenate([weight_mid, swap(weight_mid, "c")], axis=1)

    rows = lax.all_to_all(aggregated, (*PLANE, "yl"), 0, 0, tiled=True).reshape(NPLANE, 2, 2, QR, T)

    hids, hlist, htrips = pl.pallas_call(
        compact_kernel,
        out_shape=(int_list, int_list, one_int),
        in_specs=[SMEM],
        out_specs=(SMEM,) * 3,
        name="compact",
    )(hplaces)

    rows, arrived, w_in, b_in, w_mid, hids, hlist, htrips = lax.optimization_barrier(
        (rows, arrived, w_in, b_in, w_mid, hids, hlist, htrips)
    )
    hc = swap(arrived, "c")
    hy = swap(arrived, "yl")
    def project(*parts):
        groups = sum(part.shape[0] for part in parts)
        half_values = jax.ShapeDtypeStruct((2, groups, 2, QR, T), BF16)
        return pl.pallas_call(
            functools.partial(project_kernel, len(parts)),
            out_shape=(half_values, half_values),
            in_specs=[VMEM] * (len(parts) + 3),
            out_specs=(VMEM, VMEM),
            compiler_params=params(24),
            name="project",
        )(*parts, w_in, b_in, w_mid)

    behind = lax.ppermute(rows, "x", around("x", 1))
    ahead = lax.ppermute(rows, "x", around("x", -1))
    near = project(rows)
    behind, ahead, near = lax.optimization_barrier((behind, ahead, near))
    far = [
        lax.ppermute(behind[:NR], "x", around("x", 1)),
        lax.ppermute(ahead[NR:], "x", around("x", -1)),
    ]
    sides = project(behind, ahead)
    mine = [near[0], sides[0]]
    swapped = [swap(near[1], "c"), swap(sides[1], "c")]
    second_near = pl.pallas_call(
        second_near_kernel,
        out_shape=jax.ShapeDtypeStruct((2, T, T), jnp.float32),
        in_specs=[SMEM] * 5 + [HBM] + [ANY] * 4,
        out_specs=VMEM,
        scratch_shapes=[
            pltpu.VMEM((NT + 1, 2, 2, QR, T), BF16),
            pltpu.VMEM((NEAR_STEPS * LT, T, T), BF16),
            pltpu.SemaphoreType.DMA((12,)),
            pltpu.SemaphoreType.DMA((NEAR_STEPS,)),
        ],
        compiler_params=params(24),
        name="second_near",
    )(meta, trips, need, ids, places, light, *mine, *swapped)
    far, second_near = lax.optimization_barrier((far, second_near))
    far = project(*far)
    mine.append(far[0])
    swapped.append(swap(far[1], "c"))
    hy_late, _ = lax.optimization_barrier((hy, far))
    hyc = swap(hy_late, "c")
    return pl.pallas_call(
        second_kernel,
        out_shape=jax.ShapeDtypeStruct((2 * T, T), BF16),
        in_specs=[SMEM] * 7 + [HBM] + [ANY] * 4 + [VMEM] * 2 + [ANY] * 6,
        out_specs=VMEM,
        scratch_shapes=[
            pltpu.VMEM((NT + 1, 2, 2, QR, T), BF16),
            pltpu.VMEM(((NB - NEAR_STEPS) * LT, T, T), BF16),
            pltpu.VMEM((SLOTS, T, T), BF16),
            pltpu.SemaphoreType.DMA((26,)),
        ],
        compiler_params=params(24),
        name="second",
    )(
        meta, trips, htrips, ids, places, hids, hlist, light, arrived, hc, hy, hyc, second_near,
        bias_mid.reshape(1, T), *mine, *swapped,
    )


def solution(mesh):
    wide = Mesh(mesh.devices.reshape(4, 2, 8, 2, 2), ("x", "yh", "z", "yl", "c"))
    in_specs = (
        P(GROUP, None),
        P(None, FEAT),
        P(FEAT),
        P(None, FEAT),
        P(FEAT),
        P(GROUP, None, None, None, None),
        P(GROUP, None, None),
        P(GROUP, None, None),
        P(GROUP, None, None, None, None),
        P(GROUP, None, None),
        P(GROUP, None, None),
        P(GROUP),
    )
    return jax.shard_map(
        per_device, mesh=wide, in_specs=in_specs, out_specs=P(GROUP, FEAT), check_vma=False
    )
```

```python
import functools

import jax
import jax.numpy as jnp
from jax import lax
from jax.experimental import pallas as pl
from jax.experimental.pallas import tpu as pltpu
from jax.sharding import Mesh
from jax.sharding import PartitionSpec as P

BLK = ("x", "yh")
GROUP = ("x", "yh", "z")
FEAT = ("yl", "c")
PLANE = ("yh", "z")
T = 128
NB = 8
NR = 8
NG = NB * NR
NT = 2 * NG
LT = 36
HT = 8
NL = NB * LT
NH = NB * HT
SLOTS = 2 * NG
QR = T // 4
STEP = 16
NOTES = 8
NX = 4
NPLANE = 2 * NR
HSTEP = 32
NEAR_STEPS = NB - 2
FAR_AT = -(-NEAR_STEPS * LT // STEP) * STEP
LIST = FAR_AT + -(-2 * LT // STEP) * STEP
HELD = ((0, NPLANE), (NPLANE, NPLANE), (3 * NPLANE, NPLANE), (2 * NPLANE, NR), (2 * NPLANE + NR, NR))
BF16 = jnp.bfloat16
SMEM = pl.BlockSpec(memory_space=pltpu.SMEM)
VMEM = pl.BlockSpec(memory_space=pltpu.VMEM)
ANY = pl.BlockSpec(memory_space=pl.ANY)
HBM = pl.BlockSpec(memory_space=pltpu.MemorySpace.HBM)


def params(mib):
    return pltpu.CompilerParams(vmem_limit_bytes=mib * 1024 * 1024)


def turned(blk, source):
    return (((blk >> 1) - (source >> 1)) & 3) * 2 + (source & 1)

PROJECTED = ((0, 0, 0, NPLANE), (1, 0, NPLANE, NPLANE), (1, NPLANE, 3 * NPLANE, NPLANE), (2, 0, 2 * NPLANE, NPLANE))


def step_of(blk, j):
    order = j if j < 4 else (j + 2 if j < NEAR_STEPS else j - 2)
    held, y = order >> 1, order & 1
    source = (((blk >> 1) - held) & 3) * 2 + y
    return (blk - source) & (NB - 1), order * NR


def around(axis, distance):
    n = lax.axis_size(axis)
    return [(i, (i + distance) % n) for i in range(n)]


def along_x(near):
    behind = lax.ppermute(near, "x", around("x", 1))
    ahead = lax.ppermute(near, "x", around("x", -1))
    far = near.shape[0] // 2
    return [
        near,
        behind,
        ahead,
        lax.ppermute(behind[:far], "x", around("x", 1)),
        lax.ppermute(ahead[far:], "x", around("x", -1)),
    ]


def swap(x, axis):
    return lax.ppermute(x, axis, around(axis, 1))


def everyone(x, axis, n):
    spread = jnp.broadcast_to(x[None], (n, *x.shape))
    return lax.all_to_all(spread, axis, 0, 0, tiled=True)


def pack_kernel(
    meta, slots, cols, rows, lcols, heavy, out, ids, places, need, trips, quarter, seats, taken, sem
):
    blk, feat = meta[0], meta[1]
    span = pl.ds(pl.multiple_of(feat * QR, QR), QR)
    copy = pltpu.make_async_copy(heavy.at[:, span, :], quarter.at[pl.ds(0, NH)], sem)
    copy.start()
    quarter[NH] = jnp.zeros((QR, T), BF16)

    def clear(q, carry):
        taken[q] = 0
        seats[2 * q] = NH
        seats[2 * q + 1] = NH
        return carry

    lax.fori_loop(0, NG, clear, 0, unroll=8)

    def seat(i, carry):
        q = slots[0, i // HT, i % HT]
        turn = taken[q]
        taken[q] = turn + 1
        seats[2 * q + turn] = i
        return carry

    lax.fori_loop(0, NH, seat, 0, unroll=8)
    lane = lax.broadcasted_iota(jnp.int32, (NOTES, T), 1)
    copy.wait()

    def node(i):
        j = jnp.minimum(i, NH - 1)
        tile = ((blk - (j >> 3)) & (NB - 1)) * 2 * NR + cols[0, j >> 3, j & (HT - 1)]
        return jnp.where(i < NH, tile, NT)

    def fill(q, carry):
        a, b = seats[2 * q], seats[2 * q + 1]
        notes = jnp.where(lane == 0, node(a), node(b)).astype(jnp.float32).astype(BF16)
        out[q] = jnp.concatenate([quarter[a], quarter[b], notes], axis=0)
        return carry

    lax.fori_loop(0, NG, fill, 0, unroll=4)

    for g in range(FAR_AT // STEP):
        need[g] = 0

    def put(k, carry, s, start, j, base):
        n0, n1 = carry
        row, col = rows[0, s, k], lcols[0, s, k]
        at = base + jnp.where(row == 0, n0, n1)
        ids[row, at] = j * LT + k
        places[row, at] = start + (col & 1) * NG + (col >> 1)
        if base == 0:
            need[at >> 4] = j
        return n0 + 1 - row, n1 + row

    def pad(i, carry, t):
        ids[t, i] = 0
        places[t, i] = NT
        return carry

    for which, (base, blocks) in enumerate(((0, range(NEAR_STEPS)), (FAR_AT, range(NEAR_STEPS, NB)))):
        counts = (0, 0)
        for j in blocks:
            s, start = step_of(blk, j)
            counts = lax.fori_loop(
                0, LT, lambda k, c, s=s, v=start, j=j, b=base: put(k, c, s, v, j, b), counts, unroll=6
            )
        count = (jnp.maximum(counts[0], counts[1]) + STEP - 1) // STEP
        trips[which] = count
        for t in range(2):
            lax.fori_loop(base + counts[t], base + count * STEP, lambda i, c, t=t: pad(i, c, t), 0)


def compact_kernel(hplaces, ids, places, htrips):
    def clear(i, carry):
        ids[i] = 0
        places[i] = NT
        return carry

    lax.fori_loop(0, NL, clear, 0, unroll=8)

    def put(i, n):
        place = hplaces[i]
        ids[n] = i
        places[n] = place
        return n + jnp.where(place < NT, 1, 0)

    n = lax.fori_loop(0, SLOTS, put, 0, unroll=8)
    ids[n] = 0
    places[n] = NT
    htrips[0] = (n + STEP - 1) // STEP


def dots(tile, value, count, ids, places, acc):
    for u in range(0, count, 2):
        left = jnp.concatenate([tile(ids(u)), tile(ids(u + 1))], axis=1)
        right = jnp.concatenate([value(places(u)), value(places(u + 1))], axis=0)
        acc = acc + jnp.dot(left, right, preferred_element_type=jnp.float32)
    return acc


def light_copy(meta, light, tiles, j, first, rows, sem):
    step, _ = step_of(meta[0], j)
    source = light.at[pl.ds(step * LT, LT)]
    if rows is not None:
        source = light.at[pl.ds(step * LT, LT), rows, :]
    return pltpu.make_async_copy(source, tiles.at[pl.ds((j - first) * LT, LT)], sem)


def light_dots(tiles, value, ids, places, first, base, carry):
    return [
        dots(
            lambda i: tiles[jnp.maximum(i - first * LT, 0)], value, STEP,
            lambda u: ids[t, base + u], lambda u: places[t, base + u], carry[t],
        )
        for t in range(2)
    ]


def feature_copies(meta, held, parts, values, sems):
    core = meta[2]
    copies = []
    for which in range(2):
        c = core if which == 0 else 1 - core
        for (start, size), part in zip(held, parts[which * len(held) : (which + 1) * len(held)]):
            span = pl.ds(c * NG + start, size)
            copies.append(pltpu.make_async_copy(part, values.at[span], sems.at[len(copies)]))
    return copies


def first_near_kernel(meta, trips, ids, places, light, *rest):
    held = HELD[:3]
    parts, (out, values, tiles, sems) = rest[: 2 * len(held)], rest[2 * len(held) :]
    rows = pl.ds(pl.multiple_of(meta[1] * QR, QR), QR)
    copies = feature_copies(meta, held, parts, values, sems)
    for j in range(NEAR_STEPS):
        copies.append(light_copy(meta, light, tiles, j, 0, rows, sems.at[len(copies)]))
    for copy in copies:
        copy.start()
    values[NT] = jnp.zeros((T, T), BF16)
    for copy in copies:
        copy.wait()
    zero = jnp.zeros((QR, T), jnp.float32)
    body = lambda g, c: light_dots(tiles, lambda p: values[p], ids, places, 0, g * STEP, c)
    out[0], out[1] = lax.fori_loop(0, trips[0], body, [zero, zero])


def first_kernel(meta, trips, ids, places, hplaces, light, heavy, near, *rest):
    parts, (out, values, tiles, htiles, sems) = rest[: 2 * len(HELD)], rest[2 * len(HELD) :]
    owner = meta[3]
    rows = pl.ds(pl.multiple_of(meta[1] * QR, QR), QR)
    copies = feature_copies(meta, HELD, parts, values, sems)
    for j in range(NEAR_STEPS, NB):
        copies.append(light_copy(meta, light, tiles, j, NEAR_STEPS, rows, sems.at[len(copies)]))
    for slot in range(2):
        rows, span = pl.ds(slot * QR, QR), pl.ds(slot * NG, NG)
        copies.append(
            pltpu.make_async_copy(heavy.at[:, rows, :], htiles.at[span], sems.at[len(copies)])
        )
    for copy in copies:
        copy.start()
    values[NT] = jnp.zeros((T, T), BF16)
    for copy in copies:
        copy.wait()
    value = lambda p: values[p]
    body = lambda g, c: light_dots(tiles, value, ids, places, NEAR_STEPS, FAR_AT + g * STEP, c)
    sums = lax.fori_loop(0, trips[1], body, [near[0], near[1]])

    def heavy_body(g, acc):
        base = g * HSTEP
        return dots(
            lambda i: htiles[i], value, HSTEP,
            lambda u: base + u, lambda u: hplaces[base + u], acc,
        )

    hsum = lax.fori_loop(0, SLOTS // HSTEP, heavy_body, jnp.zeros((QR, T), jnp.float32))
    for t in range(2):
        total = (sums[t] + jnp.where(owner == t, hsum, 0.0)).astype(BF16)
        for n in range(2 * NPLANE):
            out[n, t] = total


def project_kernel(n, *refs):
    parts, (w_in, b_in, w_mid, mine, theirs) = refs[:n], refs[n:]
    at = 0
    for part in parts:
        size = part.shape[0]
        for rt in range(2):
            x = part[:, :, rt].reshape(-1, T)
            h = jnp.dot(x, w_in[...], preferred_element_type=jnp.float32) + b_in[...]
            h = jnp.maximum(h, 0.0).astype(BF16)
            s = jnp.dot(h, w_mid[...], preferred_element_type=jnp.float32).astype(BF16)
            mine[rt, at : at + size] = s[:, :T].reshape(size, *mine.shape[2:])
            theirs[rt, at : at + size] = s[:, T:].reshape(size, *mine.shape[2:])
        at += size


def value_copies(meta, held, parts, values, sems):
    copies = []
    for which in range(2):
        c = meta[2] if which == 0 else 1 - meta[2]
        for k, at, start, size in held:
            part = parts[which * (held[-1][0] + 1) + k]
            for rt in range(2):
                span = pl.ds(rt * NG + start, size)
                copies.append(
                    pltpu.make_async_copy(
                        part.at[rt, pl.ds(at, size)], values.at[span, :, c], sems.at[len(copies)]
                    )
                )
    return copies


def second_near_kernel(meta, trips, need, ids, places, light, *rest):
    parts, (out, values, tiles, sems, light_sems) = rest[:4], rest[4:]
    copies = value_copies(meta, PROJECTED[:3], parts, values, sems)
    chunks = [light_copy(meta, light, tiles, j, 0, None, light_sems.at[j]) for j in range(NEAR_STEPS)]
    for copy in copies + chunks:
        copy.start()
    values[NT] = jnp.zeros((2, 2, QR, T), BF16)
    for copy in copies:
        copy.wait()

    def wait_for(n):
        span = pl.ds(n * LT, LT)
        pltpu.make_async_copy(light.at[span], tiles.at[span], light_sems.at[n]).wait()
        return n + 1

    value = lambda p: values[p].reshape(T, T)

    def body(g, carry):
        here = lax.while_loop(lambda n: n <= need[g], wait_for, carry[2])
        return (*light_dots(tiles, value, ids, places, 0, g * STEP, carry[:2]), here)

    zero = jnp.zeros((T, T), jnp.float32)
    sum0, sum1, here = lax.fori_loop(0, trips[0], body, (zero, zero, 0))
    lax.while_loop(lambda n: n < NEAR_STEPS, wait_for, here)
    out[0] = sum0
    out[1] = sum1


def second_kernel(
    meta, trips, htrips, ids, places, hids, hplaces, light, h0, h1, h2, h3, near, b_mid, *rest
):
    parts, (out, values, tiles, htiles, sems) = rest[:6], rest[6:]
    feat, owner = meta[1], meta[3]
    copies = value_copies(meta, PROJECTED, parts, values, sems)
    for j in range(NEAR_STEPS, NB):
        copies.append(light_copy(meta, light, tiles, j, NEAR_STEPS, None, sems.at[len(copies)]))
    first = len(copies)
    for k, h in enumerate((h0, h1, h2, h3)):
        rows = pl.ds(pl.multiple_of((feat ^ k) * QR, QR), QR)
        for slot in range(2):
            copies.append(
                pltpu.make_async_copy(
                    h.at[:, pl.ds(slot * QR, QR), :],
                    htiles.at[pl.ds(slot * NG, NG), rows, :],
                    sems.at[len(copies)],
                )
            )
    for copy in copies:
        copy.start()
    values[NT] = jnp.zeros((2, 2, QR, T), BF16)
    for copy in copies[:first]:
        copy.wait()
    value = lambda p: values[p].reshape(T, T)
    body = lambda g, c: light_dots(tiles, value, ids, places, NEAR_STEPS, FAR_AT + g * STEP, c)
    sums = lax.fori_loop(0, trips[1], body, [near[0], near[1]])
    for copy in copies[first:]:
        copy.wait()

    def heavy_body(g, acc):
        base = g * STEP
        return dots(
            lambda i: htiles[i], value, STEP, lambda u: hids[base + u], lambda u: hplaces[base + u], acc
        )

    hsum = lax.fori_loop(0, htrips[0], heavy_body, jnp.zeros((T, T), jnp.float32))
    for t in range(2):
        total = sums[t] + jnp.where(owner == t, hsum, 0.0) + b_mid[...]
        out[t * T : (t + 1) * T] = total.astype(BF16)


def per_device(
    features, weight_in, bias_in, weight_mid, bias_mid, light_tiles, light_rows, light_cols,
    heavy_tiles, heavy_slots, heavy_cols, owner_map,
):
    i32 = jnp.int32
    blk, core, feat = lax.axis_index(BLK), lax.axis_index("c"), lax.axis_index(FEAT)
    meta = jnp.stack([blk, feat, core, owner_map[0]]).astype(i32)
    in_hbm = lambda x: pltpu.with_memory_space_constraint(x, pltpu.MemorySpace.HBM)
    light = in_hbm(light_tiles.reshape(NL, T, T))
    int_list = jax.ShapeDtypeStruct((NL,), i32)
    int_lists = jax.ShapeDtypeStruct((2, LIST), i32)
    needs = jax.ShapeDtypeStruct((FAR_AT // STEP,), i32)
    one_int = jax.ShapeDtypeStruct((1,), i32)
    two_ints = jax.ShapeDtypeStruct((2,), i32)

    half = lax.dynamic_slice_in_dim(features, core * T, T, axis=0)
    plane = everyone(half, PLANE, NPLANE)

    packed, ids, places, need, trips = pl.pallas_call(
        pack_kernel,
        out_shape=(
            jax.ShapeDtypeStruct((NG, 2 * QR + NOTES, T), BF16), int_lists, int_lists, needs, two_ints
        ),
        in_specs=[SMEM] * 5 + [HBM],
        out_specs=(VMEM, SMEM, SMEM, SMEM, SMEM),
        scratch_shapes=[
            pltpu.VMEM((NH + 1, QR, T), BF16),
            pltpu.SMEM((SLOTS,), i32),
            pltpu.SMEM((NG,), i32),
            pltpu.SemaphoreType.DMA(()),
        ],
        compiler_params=params(16),
        cost_estimate=pl.CostEstimate(flops=0, transcendentals=0, bytes_accessed=30_000_000),
        name="pack",
    )(meta, heavy_slots, heavy_cols, light_rows, light_cols, in_hbm(heavy_tiles.reshape(NH, T, T)))
    arrived = lax.all_to_all(packed, GROUP, 0, 0, tiled=True)
    own = along_x(plane)
    own, far_parts = own[:3], own[3:]
    other = [swap(part, "c") for part in own]

    nodes = arrived[:, 2 * QR, :2].T.reshape(SLOTS).astype(i32)
    hplaces = jnp.where(
        nodes < NT, (nodes & 1) * NG + turned(blk, nodes >> 4) * NR + ((nodes & 15) >> 1), NT
    )

    trips, hplaces = lax.optimization_barrier((trips, hplaces))
    first_near = pl.pallas_call(
        first_near_kernel,
        out_shape=jax.ShapeDtypeStruct((2, QR, T), jnp.float32),
        in_specs=[SMEM] * 4 + [HBM] + [ANY] * 6,
        out_specs=VMEM,
        scratch_shapes=[
            pltpu.VMEM((NT + 1, T, T), BF16),
            pltpu.VMEM((NEAR_STEPS * LT, QR, T), BF16),
            pltpu.SemaphoreType.DMA((6 + NEAR_STEPS,)),
        ],
        compiler_params=params(10),
        name="first_near",
    )(meta, trips, ids, places, light, *own, *other)
    first_near, far_parts = lax.optimization_barrier((first_near, far_parts))
    held = own + far_parts + other + [swap(part, "c") for part in far_parts]
    aggregated = pl.pallas_call(
        first_kernel,
        out_shape=jax.ShapeDtypeStruct((2 * NPLANE, 2, QR, T), BF16),
        in_specs=[SMEM] * 5 + [HBM, ANY, VMEM] + [ANY] * len(held),
        out_specs=VMEM,
        scratch_shapes=[
            pltpu.VMEM((NT + 1, T, T), BF16),
            pltpu.VMEM(((NB - NEAR_STEPS) * LT, QR, T), BF16),
            pltpu.VMEM((SLOTS, QR, T), BF16),
            pltpu.SemaphoreType.DMA((len(held) + 4,)),
        ],
        compiler_params=params(10),
        name="first",
    )(meta, trips, ids, places, hplaces, light, arrived, first_near, *held)

    aggregated, weight_in, bias_in, weight_mid = lax.optimization_barrier(
        (aggregated, weight_in, bias_in, weight_mid)
    )
    bias_rows = jnp.pad(bias_in.reshape(1, T), ((0, 7), (0, 0)))
    pieces = jnp.concatenate([weight_in.astype(jnp.float32), bias_rows], axis=0)
    pieces = jnp.stack([pieces, swap(pieces, "yl")])
    pieces = jnp.stack([pieces, swap(pieces, "c")], axis=1).reshape(4, T + 8, T)
    pieces = jnp.take(pieces, feat ^ jnp.arange(4), axis=0)
    w_in = jnp.moveaxis(pieces[:, :T], 0, 1).reshape(T, 4 * T).astype(BF16)
    b_in = pieces[:, T].reshape(1, 4 * T)
    w_mid = jnp.concatenate([weight_mid, swap(weight_mid, "c")], axis=1)

    rows = lax.all_to_all(aggregated, (*PLANE, "yl"), 0, 0, tiled=True).reshape(NPLANE, 2, 2, QR, T)

    hids, hlist, htrips = pl.pallas_call(
        compact_kernel,
        out_shape=(int_list, int_list, one_int),
        in_specs=[SMEM],
        out_specs=(SMEM,) * 3,
        name="compact",
    )(hplaces)

    rows, arrived, w_in, b_in, w_mid, hids, hlist, htrips = lax.optimization_barrier(
        (rows, arrived, w_in, b_in, w_mid, hids, hlist, htrips)
    )
    hc = swap(arrived, "c")
    hy = swap(arrived, "yl")
    def project(*parts):
        groups = sum(part.shape[0] for part in parts)
        half_values = jax.ShapeDtypeStruct((2, groups, 2, QR, T), BF16)
        return pl.pallas_call(
            functools.partial(project_kernel, len(parts)),
            out_shape=(half_values, half_values),
            in_specs=[VMEM] * (len(parts) + 3),
            out_specs=(VMEM, VMEM),
            compiler_params=params(12),
            name="project",
        )(*parts, w_in, b_in, w_mid)

    behind = lax.ppermute(rows, "x", around("x", 1))
    ahead = lax.ppermute(rows, "x", around("x", -1))
    near = project(rows)
    behind, ahead, near = lax.optimization_barrier((behind, ahead, near))
    far = [
        lax.ppermute(behind[:NR], "x", around("x", 1)),
        lax.ppermute(ahead[NR:], "x", around("x", -1)),
    ]
    sides = project(behind, ahead)
    mine = [near[0], sides[0]]
    swapped = [swap(near[1], "c"), swap(sides[1], "c")]
    second_near = pl.pallas_call(
        second_near_kernel,
        out_shape=jax.ShapeDtypeStruct((2, T, T), jnp.float32),
        in_specs=[SMEM] * 5 + [HBM] + [ANY] * 4,
        out_specs=VMEM,
        scratch_shapes=[
            pltpu.VMEM((NT + 1, 2, 2, QR, T), BF16),
            pltpu.VMEM((NEAR_STEPS * LT, T, T), BF16),
            pltpu.SemaphoreType.DMA((12,)),
            pltpu.SemaphoreType.DMA((NEAR_STEPS,)),
        ],
        compiler_params=params(16),
        name="second_near",
    )(meta, trips, need, ids, places, light, *mine, *swapped)
    far, second_near = lax.optimization_barrier((far, second_near))
    far = project(*far)
    mine.append(far[0])
    swapped.append(swap(far[1], "c"))
    hy_late, _ = lax.optimization_barrier((hy, far))
    hyc = swap(hy_late, "c")
    return pl.pallas_call(
        second_kernel,
        out_shape=jax.ShapeDtypeStruct((2 * T, T), BF16),
        in_specs=[SMEM] * 7 + [HBM] + [ANY] * 4 + [VMEM] * 2 + [ANY] * 6,
        out_specs=VMEM,
        scratch_shapes=[
            pltpu.VMEM((NT + 1, 2, 2, QR, T), BF16),
            pltpu.VMEM(((NB - NEAR_STEPS) * LT, T, T), BF16),
            pltpu.VMEM((SLOTS, T, T), BF16),
            pltpu.SemaphoreType.DMA((26,)),
        ],
        compiler_params=params(16),
        name="second",
    )(
        meta, trips, htrips, ids, places, hids, hlist, light, arrived, hc, hy, hyc, second_near,
        bias_mid.reshape(1, T), *mine, *swapped,
    )


def solution(mesh):
    wide = Mesh(mesh.devices.reshape(4, 2, 8, 2, 2), ("x", "yh", "z", "yl", "c"))
    in_specs = (
        P(GROUP, None),
        P(None, FEAT),
        P(FEAT),
        P(None, FEAT),
        P(FEAT),
        P(GROUP, None, None, None, None),
        P(GROUP, None, None),
        P(GROUP, None, None),
        P(GROUP, None, None, None, None),
        P(GROUP, None, None),
        P(GROUP, None, None),
        P(GROUP),
    )
    return jax.shard_map(
        per_device, mesh=wide, in_specs=in_specs, out_specs=P(GROUP, FEAT), check_vma=False
    )
```

```python
import functools

import jax
import jax.numpy as jnp
from jax import lax
from jax.experimental import pallas as pl
from jax.experimental.pallas import tpu as pltpu
from jax.sharding import Mesh
from jax.sharding import PartitionSpec as P

BLK = ("x", "yh")
GROUP = ("x", "yh", "z")
FEAT = ("yl", "c")
PLANE = ("yh", "z")
T = 128
NB = 8
NR = 8
NG = NB * NR
NT = 2 * NG
LT = 36
HT = 8
NL = NB * LT
NH = NB * HT
SLOTS = 2 * NG
QR = T // 4
STEP = 16
NOTES = 8
NX = 4
NPLANE = 2 * NR
HSTEP = 32
NEAR_STEPS = NB - 2
FAR_AT = -(-NEAR_STEPS * LT // STEP) * STEP
LIST = FAR_AT + -(-2 * LT // STEP) * STEP
HELD = ((0, NPLANE), (NPLANE, NPLANE), (3 * NPLANE, NPLANE), (2 * NPLANE, NR), (2 * NPLANE + NR, NR))
BF16 = jnp.bfloat16
SMEM = pl.BlockSpec(memory_space=pltpu.SMEM)
VMEM = pl.BlockSpec(memory_space=pltpu.VMEM)
ANY = pl.BlockSpec(memory_space=pl.ANY)
HBM = pl.BlockSpec(memory_space=pltpu.MemorySpace.HBM)


def params(mib):
    return pltpu.CompilerParams(vmem_limit_bytes=mib * 1024 * 1024)


def turned(blk, source):
    return (((blk >> 1) - (source >> 1)) & 3) * 2 + (source & 1)

PROJECTED = ((0, 0, 0, NPLANE), (1, 0, NPLANE, NPLANE), (1, NPLANE, 3 * NPLANE, NPLANE), (2, 0, 2 * NPLANE, NPLANE))


def step_of(blk, j):
    order = j if j < 4 else (j + 2 if j < NEAR_STEPS else j - 2)
    held, y = order >> 1, order & 1
    source = (((blk >> 1) - held) & 3) * 2 + y
    return (blk - source) & (NB - 1), order * NR


def around(axis, distance):
    n = lax.axis_size(axis)
    return [(i, (i + distance) % n) for i in range(n)]


def along_x(near):
    behind = lax.ppermute(near, "x", around("x", 1))
    ahead = lax.ppermute(near, "x", around("x", -1))
    far = near.shape[0] // 2
    return [
        near,
        behind,
        ahead,
        lax.ppermute(behind[:far], "x", around("x", 1)),
        lax.ppermute(ahead[far:], "x", around("x", -1)),
    ]


def swap(x, axis):
    return lax.ppermute(x, axis, around(axis, 1))


def everyone(x, axis, n):
    spread = jnp.broadcast_to(x[None], (n, *x.shape))
    return lax.all_to_all(spread, axis, 0, 0, tiled=True)


def pack_kernel(
    meta, slots, cols, rows, lcols, heavy, out, ids, places, need, trips, quarter, seats, taken, sem
):
    blk, feat = meta[0], meta[1]
    span = pl.ds(pl.multiple_of(feat * QR, QR), QR)
    copy = pltpu.make_async_copy(heavy.at[:, span, :], quarter.at[pl.ds(0, NH)], sem)
    copy.start()
    quarter[NH] = jnp.zeros((QR, T), BF16)

    def clear(q, carry):
        taken[q] = 0
        seats[2 * q] = NH
        seats[2 * q + 1] = NH
        return carry

    lax.fori_loop(0, NG, clear, 0, unroll=8)

    def seat(i, carry):
        q = slots[0, i // HT, i % HT]
        turn = taken[q]
        taken[q] = turn + 1
        seats[2 * q + turn] = i
        return carry

    lax.fori_loop(0, NH, seat, 0, unroll=8)
    lane = lax.broadcasted_iota(jnp.int32, (NOTES, T), 1)
    copy.wait()

    def node(i):
        j = jnp.minimum(i, NH - 1)
        tile = ((blk - (j >> 3)) & (NB - 1)) * 2 * NR + cols[0, j >> 3, j & (HT - 1)]
        return jnp.where(i < NH, tile, NT)

    def fill(q, carry):
        a, b = seats[2 * q], seats[2 * q + 1]
        notes = jnp.where(lane == 0, node(a), node(b)).astype(jnp.float32).astype(BF16)
        out[q] = jnp.concatenate([quarter[a], quarter[b], notes], axis=0)
        return carry

    lax.fori_loop(0, NG, fill, 0, unroll=4)

    for g in range(FAR_AT // STEP):
        need[g] = 0

    def put(k, carry, s, start, j, base):
        n0, n1 = carry
        row, col = rows[0, s, k], lcols[0, s, k]
        at = base + jnp.where(row == 0, n0, n1)
        ids[row, at] = j * LT + k
        places[row, at] = start + (col & 1) * NG + (col >> 1)
        if base == 0:
            need[at >> 4] = j
        return n0 + 1 - row, n1 + row

    def pad(i, carry, t):
        ids[t, i] = 0
        places[t, i] = NT
        return carry

    for which, (base, blocks) in enumerate(((0, range(NEAR_STEPS)), (FAR_AT, range(NEAR_STEPS, NB)))):
        counts = (0, 0)
        for j in blocks:
            s, start = step_of(blk, j)
            counts = lax.fori_loop(
                0, LT, lambda k, c, s=s, v=start, j=j, b=base: put(k, c, s, v, j, b), counts, unroll=6
            )
        count = (jnp.maximum(counts[0], counts[1]) + STEP - 1) // STEP
        trips[which] = count
        for t in range(2):
            lax.fori_loop(base + counts[t], base + count * STEP, lambda i, c, t=t: pad(i, c, t), 0)


def compact_kernel(hplaces, ids, places, htrips):
    def clear(i, carry):
        ids[i] = 0
        places[i] = NT
        return carry

    lax.fori_loop(0, NL, clear, 0, unroll=8)

    def put(i, n):
        place = hplaces[i]
        ids[n] = i
        places[n] = place
        return n + jnp.where(place < NT, 1, 0)

    n = lax.fori_loop(0, SLOTS, put, 0, unroll=8)
    ids[n] = 0
    places[n] = NT
    htrips[0] = (n + STEP - 1) // STEP


def dots(tile, value, count, ids, places, acc):
    for u in range(0, count, 2):
        left = jnp.concatenate([tile(ids(u)), tile(ids(u + 1))], axis=1)
        right = jnp.concatenate([value(places(u)), value(places(u + 1))], axis=0)
        acc = acc + jnp.dot(left, right, preferred_element_type=jnp.float32)
    return acc


def light_copy(meta, light, tiles, j, first, rows, sem):
    step, _ = step_of(meta[0], j)
    source = light.at[pl.ds(step * LT, LT)]
    if rows is not None:
        source = light.at[pl.ds(step * LT, LT), rows, :]
    return pltpu.make_async_copy(source, tiles.at[pl.ds((j - first) * LT, LT)], sem)


def light_dots(tiles, value, ids, places, first, base, carry):
    return [
        dots(
            lambda i: tiles[jnp.maximum(i - first * LT, 0)], value, STEP,
            lambda u: ids[t, base + u], lambda u: places[t, base + u], carry[t],
        )
        for t in range(2)
    ]


def feature_copies(meta, held, parts, values, sems):
    core = meta[2]
    copies = []
    for which in range(2):
        c = core if which == 0 else 1 - core
        for (start, size), part in zip(held, parts[which * len(held) : (which + 1) * len(held)]):
            span = pl.ds(c * NG + start, size)
            copies.append(pltpu.make_async_copy(part, values.at[span], sems.at[len(copies)]))
    return copies


def first_near_kernel(meta, trips, ids, places, light, *rest):
    held = HELD[:3]
    parts, (out, values, tiles, sems) = rest[: 2 * len(held)], rest[2 * len(held) :]
    rows = pl.ds(pl.multiple_of(meta[1] * QR, QR), QR)
    copies = feature_copies(meta, held, parts, values, sems)
    for j in range(NEAR_STEPS):
        copies.append(light_copy(meta, light, tiles, j, 0, rows, sems.at[len(copies)]))
    for copy in copies:
        copy.start()
    values[NT] = jnp.zeros((T, T), BF16)
    for copy in copies:
        copy.wait()
    zero = jnp.zeros((QR, T), jnp.float32)
    body = lambda g, c: light_dots(tiles, lambda p: values[p], ids, places, 0, g * STEP, c)
    out[0], out[1] = lax.fori_loop(0, trips[0], body, [zero, zero])


def first_kernel(meta, trips, ids, places, hplaces, light, heavy, near, *rest):
    parts, (out, values, tiles, htiles, sems) = rest[: 2 * len(HELD)], rest[2 * len(HELD) :]
    owner = meta[3]
    rows = pl.ds(pl.multiple_of(meta[1] * QR, QR), QR)
    copies = feature_copies(meta, HELD, parts, values, sems)
    for j in range(NEAR_STEPS, NB):
        copies.append(light_copy(meta, light, tiles, j, NEAR_STEPS, rows, sems.at[len(copies)]))
    for slot in range(2):
        rows, span = pl.ds(slot * QR, QR), pl.ds(slot * NG, NG)
        copies.append(
            pltpu.make_async_copy(heavy.at[:, rows, :], htiles.at[span], sems.at[len(copies)])
        )
    for copy in copies:
        copy.start()
    values[NT] = jnp.zeros((T, T), BF16)
    for copy in copies:
        copy.wait()
    value = lambda p: values[p]
    body = lambda g, c: light_dots(tiles, value, ids, places, NEAR_STEPS, FAR_AT + g * STEP, c)
    sums = lax.fori_loop(0, trips[1], body, [near[0], near[1]])

    def heavy_body(g, acc):
        base = g * HSTEP
        return dots(
            lambda i: htiles[i], value, HSTEP,
            lambda u: base + u, lambda u: hplaces[base + u], acc,
        )

    hsum = lax.fori_loop(0, SLOTS // HSTEP, heavy_body, jnp.zeros((QR, T), jnp.float32))
    for t in range(2):
        total = (sums[t] + jnp.where(owner == t, hsum, 0.0)).astype(BF16)
        for n in range(2 * NR):
            out[n, t] = total


def project_kernel(across, n, meta, *refs):
    parts, (w_in, b_in, w_mid, mine, theirs) = refs[:n], refs[n:]
    y = meta[0] & 1
    at = 0
    for part, first in zip(parts, across):
        size = part.shape[0]
        for k in range(size):
            group = pl.ds(at + jnp.bitwise_xor(y, k + first) * NR, NR)
            x = part[k].reshape(-1, T)
            h = jnp.dot(x, w_in[...], preferred_element_type=jnp.float32) + b_in[...]
            h = jnp.maximum(h, 0.0).astype(BF16)
            s = jnp.dot(h, w_mid[...], preferred_element_type=jnp.float32).astype(BF16)
            s = s.reshape(NR, 2, 2, QR, 2 * T)
            for rt in range(2):
                mine[rt, group] = s[:, :, rt, :, :T]
                theirs[rt, group] = s[:, :, rt, :, T:]
        if size == 2:
            at += NPLANE


def value_copies(meta, held, parts, values, sems):
    copies = []
    for which in range(2):
        c = meta[2] if which == 0 else 1 - meta[2]
        for k, at, start, size in held:
            part = parts[which * (held[-1][0] + 1) + k]
            for rt in range(2):
                span = pl.ds(rt * NG + start, size)
                copies.append(
                    pltpu.make_async_copy(
                        part.at[rt, pl.ds(at, size)], values.at[span, :, c], sems.at[len(copies)]
                    )
                )
    return copies


def second_near_kernel(meta, trips, need, ids, places, light, *rest):
    parts, (out, values, tiles, sems, light_sems) = rest[:4], rest[4:]
    copies = value_copies(meta, PROJECTED[:3], parts, values, sems)
    chunks = [light_copy(meta, light, tiles, j, 0, None, light_sems.at[j]) for j in range(NEAR_STEPS)]
    for copy in copies + chunks:
        copy.start()
    values[NT] = jnp.zeros((2, 2, QR, T), BF16)
    for copy in copies:
        copy.wait()

    def wait_for(n):
        span = pl.ds(n * LT, LT)
        pltpu.make_async_copy(light.at[span], tiles.at[span], light_sems.at[n]).wait()
        return n + 1

    value = lambda p: values[p].reshape(T, T)

    def body(g, carry):
        here = lax.while_loop(lambda n: n <= need[g], wait_for, carry[2])
        return (*light_dots(tiles, value, ids, places, 0, g * STEP, carry[:2]), here)

    zero = jnp.zeros((T, T), jnp.float32)
    sum0, sum1, here = lax.fori_loop(0, trips[0], body, (zero, zero, 0))
    lax.while_loop(lambda n: n < NEAR_STEPS, wait_for, here)
    out[0] = sum0
    out[1] = sum1


def second_kernel(
    meta, trips, htrips, ids, places, hids, hplaces, light, h0, h1, h2, h3, near, b_mid, *rest
):
    parts, (out, values, tiles, htiles, sems) = rest[:6], rest[6:]
    feat, owner = meta[1], meta[3]
    copies = value_copies(meta, PROJECTED, parts, values, sems)
    for j in range(NEAR_STEPS, NB):
        copies.append(light_copy(meta, light, tiles, j, NEAR_STEPS, None, sems.at[len(copies)]))
    first = len(copies)
    for k, h in enumerate((h0, h1, h2, h3)):
        rows = pl.ds(pl.multiple_of((feat ^ k) * QR, QR), QR)
        for slot in range(2):
            copies.append(
                pltpu.make_async_copy(
                    h.at[:, pl.ds(slot * QR, QR), :],
                    htiles.at[pl.ds(slot * NG, NG), rows, :],
                    sems.at[len(copies)],
                )
            )
    for copy in copies:
        copy.start()
    values[NT] = jnp.zeros((2, 2, QR, T), BF16)
    for copy in copies[:first]:
        copy.wait()
    value = lambda p: values[p].reshape(T, T)
    body = lambda g, c: light_dots(tiles, value, ids, places, NEAR_STEPS, FAR_AT + g * STEP, c)
    sums = lax.fori_loop(0, trips[1], body, [near[0], near[1]])
    for copy in copies[first:]:
        copy.wait()

    def heavy_body(g, acc):
        base = g * STEP
        return dots(
            lambda i: htiles[i], value, STEP, lambda u: hids[base + u], lambda u: hplaces[base + u], acc
        )

    hsum = lax.fori_loop(0, htrips[0], heavy_body, jnp.zeros((T, T), jnp.float32))
    for t in range(2):
        total = sums[t] + jnp.where(owner == t, hsum, 0.0) + b_mid[...]
        out[t * T : (t + 1) * T] = total.astype(BF16)


def per_device(
    features, weight_in, bias_in, weight_mid, bias_mid, light_tiles, light_rows, light_cols,
    heavy_tiles, heavy_slots, heavy_cols, owner_map,
):
    i32 = jnp.int32
    blk, core, feat = lax.axis_index(BLK), lax.axis_index("c"), lax.axis_index(FEAT)
    meta = jnp.stack([blk, feat, core, owner_map[0]]).astype(i32)
    in_hbm = lambda x: pltpu.with_memory_space_constraint(x, pltpu.MemorySpace.HBM)
    light = in_hbm(light_tiles.reshape(NL, T, T))
    int_list = jax.ShapeDtypeStruct((NL,), i32)
    int_lists = jax.ShapeDtypeStruct((2, LIST), i32)
    needs = jax.ShapeDtypeStruct((FAR_AT // STEP,), i32)
    one_int = jax.ShapeDtypeStruct((1,), i32)
    two_ints = jax.ShapeDtypeStruct((2,), i32)

    half = lax.dynamic_slice_in_dim(features, core * T, T, axis=0)
    plane = everyone(half, PLANE, NPLANE)

    packed, ids, places, need, trips = pl.pallas_call(
        pack_kernel,
        out_shape=(
            jax.ShapeDtypeStruct((NG, 2 * QR + NOTES, T), BF16), int_lists, int_lists, needs, two_ints
        ),
        in_specs=[SMEM] * 5 + [HBM],
        out_specs=(VMEM, SMEM, SMEM, SMEM, SMEM),
        scratch_shapes=[
            pltpu.VMEM((NH + 1, QR, T), BF16),
            pltpu.SMEM((SLOTS,), i32),
            pltpu.SMEM((NG,), i32),
            pltpu.SemaphoreType.DMA(()),
        ],
        compiler_params=params(16),
        cost_estimate=pl.CostEstimate(flops=0, transcendentals=0, bytes_accessed=30_000_000),
        name="pack",
    )(meta, heavy_slots, heavy_cols, light_rows, light_cols, in_hbm(heavy_tiles.reshape(NH, T, T)))
    arrived = lax.all_to_all(packed, GROUP, 0, 0, tiled=True)
    own = along_x(plane)
    own, far_parts = own[:3], own[3:]
    other = [swap(part, "c") for part in own]

    nodes = arrived[:, 2 * QR, :2].T.reshape(SLOTS).astype(i32)
    hplaces = jnp.where(
        nodes < NT, (nodes & 1) * NG + turned(blk, nodes >> 4) * NR + ((nodes & 15) >> 1), NT
    )

    trips, hplaces = lax.optimization_barrier((trips, hplaces))
    first_near = pl.pallas_call(
        first_near_kernel,
        out_shape=jax.ShapeDtypeStruct((2, QR, T), jnp.float32),
        in_specs=[SMEM] * 4 + [HBM] + [ANY] * 6,
        out_specs=VMEM,
        scratch_shapes=[
            pltpu.VMEM((NT + 1, T, T), BF16),
            pltpu.VMEM((NEAR_STEPS * LT, QR, T), BF16),
            pltpu.SemaphoreType.DMA((6 + NEAR_STEPS,)),
        ],
        compiler_params=params(10),
        name="first_near",
    )(meta, trips, ids, places, light, *own, *other)
    first_near, far_parts = lax.optimization_barrier((first_near, far_parts))
    held = own + far_parts + other + [swap(part, "c") for part in far_parts]
    aggregated = pl.pallas_call(
        first_kernel,
        out_shape=jax.ShapeDtypeStruct((2 * NR, 2, QR, T), BF16),
        in_specs=[SMEM] * 5 + [HBM, ANY, VMEM] + [ANY] * len(held),
        out_specs=VMEM,
        scratch_shapes=[
            pltpu.VMEM((NT + 1, T, T), BF16),
            pltpu.VMEM(((NB - NEAR_STEPS) * LT, QR, T), BF16),
            pltpu.VMEM((SLOTS, QR, T), BF16),
            pltpu.SemaphoreType.DMA((len(held) + 4,)),
        ],
        compiler_params=params(10),
        name="first",
    )(meta, trips, ids, places, hplaces, light, arrived, first_near, *held)

    aggregated, weight_in, bias_in, weight_mid = lax.optimization_barrier(
        (aggregated, weight_in, bias_in, weight_mid)
    )
    bias_rows = jnp.pad(bias_in.reshape(1, T), ((0, 7), (0, 0)))
    pieces = jnp.concatenate([weight_in.astype(jnp.float32), bias_rows], axis=0)
    pieces = jnp.stack([pieces, swap(pieces, "yl")])
    pieces = jnp.stack([pieces, swap(pieces, "c")], axis=1).reshape(4, T + 8, T)
    pieces = jnp.take(pieces, feat ^ jnp.arange(4), axis=0)
    w_in = jnp.moveaxis(pieces[:, :T], 0, 1).reshape(T, 4 * T).astype(BF16)
    b_in = pieces[:, T].reshape(1, 4 * T)
    w_mid = jnp.concatenate([weight_mid, swap(weight_mid, "c")], axis=1)

    column = lax.all_to_all(aggregated, ("z", "yl"), 0, 0, tiled=True).reshape(NR, 2, 2, QR, T)
    rows = jnp.stack([column, swap(column, "yh")])

    hids, hlist, htrips = pl.pallas_call(
        compact_kernel,
        out_shape=(int_list, int_list, one_int),
        in_specs=[SMEM],
        out_specs=(SMEM,) * 3,
        name="compact",
    )(hplaces)

    rows, arrived, w_in, b_in, w_mid, hids, hlist, htrips = lax.optimization_barrier(
        (rows, arrived, w_in, b_in, w_mid, hids, hlist, htrips)
    )
    hc = swap(arrived, "c")
    hy = swap(arrived, "yl")
    def project(parts, across):
        groups = sum(part.shape[0] for part in parts) * NR
        half_values = jax.ShapeDtypeStruct((2, groups, 2, QR, T), BF16)
        return pl.pallas_call(
            functools.partial(project_kernel, across, len(parts)),
            out_shape=(half_values, half_values),
            in_specs=[SMEM] + [VMEM] * (len(parts) + 3),
            out_specs=(VMEM, VMEM),
            compiler_params=params(12),
            name="project",
        )(meta, *parts, w_in, b_in, w_mid)

    behind = lax.ppermute(rows, "x", around("x", 1))
    ahead = lax.ppermute(rows, "x", around("x", -1))
    near = project([rows], (0,))
    behind, ahead, near = lax.optimization_barrier((behind, ahead, near))
    far = [
        lax.ppermute(behind[:1], "x", around("x", 1)),
        lax.ppermute(ahead[1:], "x", around("x", -1)),
    ]
    sides = project([behind, ahead], (0, 0))
    mine = [near[0], sides[0]]
    swapped = [swap(near[1], "c"), swap(sides[1], "c")]
    second_near = pl.pallas_call(
        second_near_kernel,
        out_shape=jax.ShapeDtypeStruct((2, T, T), jnp.float32),
        in_specs=[SMEM] * 5 + [HBM] + [ANY] * 4,
        out_specs=VMEM,
        scratch_shapes=[
            pltpu.VMEM((NT + 1, 2, 2, QR, T), BF16),
            pltpu.VMEM((NEAR_STEPS * LT, T, T), BF16),
            pltpu.SemaphoreType.DMA((12,)),
            pltpu.SemaphoreType.DMA((NEAR_STEPS,)),
        ],
        compiler_params=params(16),
        name="second_near",
    )(meta, trips, need, ids, places, light, *mine, *swapped)
    far, second_near = lax.optimization_barrier((far, second_near))
    far = project(far, (0, 1))
    mine.append(far[0])
    swapped.append(swap(far[1], "c"))
    hy_late, _ = lax.optimization_barrier((hy, far))
    hyc = swap(hy_late, "c")
    return pl.pallas_call(
        second_kernel,
        out_shape=jax.ShapeDtypeStruct((2 * T, T), BF16),
        in_specs=[SMEM] * 7 + [HBM] + [ANY] * 4 + [VMEM] * 2 + [ANY] * 6,
        out_specs=VMEM,
        scratch_shapes=[
            pltpu.VMEM((NT + 1, 2, 2, QR, T), BF16),
            pltpu.VMEM(((NB - NEAR_STEPS) * LT, T, T), BF16),
            pltpu.VMEM((SLOTS, T, T), BF16),
            pltpu.SemaphoreType.DMA((26,)),
        ],
        compiler_params=params(16),
        name="second",
    )(
        meta, trips, htrips, ids, places, hids, hlist, light, arrived, hc, hy, hyc, second_near,
        bias_mid.reshape(1, T), *mine, *swapped,
    )


def solution(mesh):
    wide = Mesh(mesh.devices.reshape(4, 2, 8, 2, 2), ("x", "yh", "z", "yl", "c"))
    in_specs = (
        P(GROUP, None),
        P(None, FEAT),
        P(FEAT),
        P(None, FEAT),
        P(FEAT),
        P(GROUP, None, None, None, None),
        P(GROUP, None, None),
        P(GROUP, None, None),
        P(GROUP, None, None, None, None),
        P(GROUP, None, None),
        P(GROUP, None, None),
        P(GROUP),
    )
    return jax.shard_map(
        per_device, mesh=wide, in_specs=in_specs, out_specs=P(GROUP, FEAT), check_vma=False
    )
```

```python
import functools

import jax
import jax.numpy as jnp
from jax import lax
from jax.experimental import pallas as pl
from jax.experimental.pallas import tpu as pltpu
from jax.sharding import Mesh
from jax.sharding import PartitionSpec as P

BLK = ("x", "yh")
GROUP = ("x", "yh", "z")
FEAT = ("yl", "c")
PLANE = ("yh", "z")
T = 128
NB = 8
NR = 8
NG = NB * NR
NT = 2 * NG
LT = 36
HT = 8
NL = NB * LT
NH = NB * HT
SLOTS = 2 * NG
QR = T // 4
STEP = 16
NOTES = 8
NX = 4
NPLANE = 2 * NR
HSTEP = 64
HLIST_STEP = 32
NEAR_STEPS = NB - 2
FAR_AT = -(-NEAR_STEPS * LT // STEP) * STEP
LIST = FAR_AT + -(-2 * LT // STEP) * STEP
HELD = ((0, NPLANE), (NPLANE, NPLANE), (3 * NPLANE, NPLANE), (2 * NPLANE, NR), (2 * NPLANE + NR, NR))
BF16 = jnp.bfloat16
SMEM = pl.BlockSpec(memory_space=pltpu.SMEM)
VMEM = pl.BlockSpec(memory_space=pltpu.VMEM)
ANY = pl.BlockSpec(memory_space=pl.ANY)
HBM = pl.BlockSpec(memory_space=pltpu.MemorySpace.HBM)


def params(mib):
    return pltpu.CompilerParams(vmem_limit_bytes=mib * 1024 * 1024)


def turned(blk, source):
    return (((blk >> 1) - (source >> 1)) & 3) * 2 + (source & 1)

PROJECTED = ((0, 0, 0, NPLANE), (1, 0, NPLANE, NPLANE), (1, NPLANE, 3 * NPLANE, NPLANE), (2, 0, 2 * NPLANE, NPLANE))


def step_of(blk, j):
    order = j if j < 4 else (j + 2 if j < NEAR_STEPS else j - 2)
    held, y = order >> 1, order & 1
    source = (((blk >> 1) - held) & 3) * 2 + y
    return (blk - source) & (NB - 1), order * NR


def around(axis, distance):
    n = lax.axis_size(axis)
    return [(i, (i + distance) % n) for i in range(n)]


def along_x(near):
    behind = lax.ppermute(near, "x", around("x", 1))
    ahead = lax.ppermute(near, "x", around("x", -1))
    far = near.shape[0] // 2
    return [
        near,
        behind,
        ahead,
        lax.ppermute(behind[:far], "x", around("x", 1)),
        lax.ppermute(ahead[far:], "x", around("x", -1)),
    ]


def swap(x, axis):
    return lax.ppermute(x, axis, around(axis, 1))


def everyone(x, axis, n):
    spread = jnp.broadcast_to(x[None], (n, *x.shape))
    return lax.all_to_all(spread, axis, 0, 0, tiled=True)


def pack_kernel(
    meta, slots, cols, rows, lcols, heavy, out, ids, places, need, trips, quarter, seats, taken, sem
):
    blk, feat = meta[0], meta[1]
    span = pl.ds(pl.multiple_of(feat * QR, QR), QR)
    copy = pltpu.make_async_copy(heavy.at[:, span, :], quarter.at[pl.ds(0, NH)], sem)
    copy.start()
    quarter[NH] = jnp.zeros((QR, T), BF16)

    def clear(q, carry):
        taken[q] = 0
        seats[2 * q] = NH
        seats[2 * q + 1] = NH
        return carry

    lax.fori_loop(0, NG, clear, 0, unroll=8)

    def seat(i, carry):
        q = slots[0, i // HT, i % HT]
        turn = taken[q]
        taken[q] = turn + 1
        seats[2 * q + turn] = i
        return carry

    lax.fori_loop(0, NH, seat, 0, unroll=8)
    lane = lax.broadcasted_iota(jnp.int32, (NOTES, T), 1)
    copy.wait()

    def node(i):
        j = jnp.minimum(i, NH - 1)
        tile = ((blk - (j >> 3)) & (NB - 1)) * 2 * NR + cols[0, j >> 3, j & (HT - 1)]
        return jnp.where(i < NH, tile, NT)

    def fill(q, carry):
        a, b = seats[2 * q], seats[2 * q + 1]
        notes = jnp.where(lane == 0, node(a), node(b)).astype(jnp.float32).astype(BF16)
        out[q] = jnp.concatenate([quarter[a], quarter[b], notes], axis=0)
        return carry

    lax.fori_loop(0, NG, fill, 0, unroll=4)

    for g in range(FAR_AT // STEP):
        need[g] = 0

    def put(k, carry, s, start, j, base):
        n0, n1 = carry
        row, col = rows[0, s, k], lcols[0, s, k]
        at = base + jnp.where(row == 0, n0, n1)
        ids[row, at] = j * LT + k
        places[row, at] = start + (col & 1) * NG + (col >> 1)
        if base == 0:
            need[at >> 4] = j
        return n0 + 1 - row, n1 + row

    def pad(i, carry, t):
        ids[t, i] = 0
        places[t, i] = NT
        return carry

    for which, (base, blocks) in enumerate(((0, range(NEAR_STEPS)), (FAR_AT, range(NEAR_STEPS, NB)))):
        counts = (0, 0)
        for j in blocks:
            s, start = step_of(blk, j)
            counts = lax.fori_loop(
                0, LT, lambda k, c, s=s, v=start, j=j, b=base: put(k, c, s, v, j, b), counts, unroll=6
            )
        count = (jnp.maximum(counts[0], counts[1]) + STEP - 1) // STEP
        trips[which] = count
        for t in range(2):
            lax.fori_loop(base + counts[t], base + count * STEP, lambda i, c, t=t: pad(i, c, t), 0)


def compact_kernel(hplaces, ids, places, htrips):
    def clear(i, carry):
        ids[i] = 0
        places[i] = NT
        return carry

    lax.fori_loop(0, NL, clear, 0, unroll=8)

    def put(i, n):
        place = hplaces[i]
        ids[n] = i
        places[n] = place
        return n + jnp.where(place < NT, 1, 0)

    n = lax.fori_loop(0, SLOTS, put, 0, unroll=8)
    ids[n] = 0
    places[n] = NT
    htrips[0] = (n + HLIST_STEP - 1) // HLIST_STEP


def dots(tile, value, count, ids, places, acc):
    for u in range(0, count, 2):
        left = jnp.concatenate([tile(ids(u)), tile(ids(u + 1))], axis=1)
        right = jnp.concatenate([value(places(u)), value(places(u + 1))], axis=0)
        acc = acc + jnp.dot(left, right, preferred_element_type=jnp.float32)
    return acc


def light_copy(meta, light, tiles, j, first, rows, sem):
    step, _ = step_of(meta[0], j)
    source = light.at[pl.ds(step * LT, LT)]
    if rows is not None:
        source = light.at[pl.ds(step * LT, LT), rows, :]
    return pltpu.make_async_copy(source, tiles.at[pl.ds((j - first) * LT, LT)], sem)


def light_dots(tiles, value, ids, places, first, base, carry):
    return [
        dots(
            lambda i: tiles[jnp.maximum(i - first * LT, 0)], value, STEP,
            lambda u: ids[t, base + u], lambda u: places[t, base + u], carry[t],
        )
        for t in range(2)
    ]


def feature_copies(meta, held, parts, values, sems):
    core = meta[2]
    copies = []
    for which in range(2):
        c = core if which == 0 else 1 - core
        for (start, size), part in zip(held, parts[which * len(held) : (which + 1) * len(held)]):
            span = pl.ds(c * NG + start, size)
            copies.append(pltpu.make_async_copy(part, values.at[span], sems.at[len(copies)]))
    return copies


def first_near_kernel(meta, trips, ids, places, light, *rest):
    held = HELD[:3]
    parts, (out, values, tiles, sems) = rest[: 2 * len(held)], rest[2 * len(held) :]
    rows = pl.ds(pl.multiple_of(meta[1] * QR, QR), QR)
    copies = feature_copies(meta, held, parts, values, sems)
    for j in range(NEAR_STEPS):
        copies.append(light_copy(meta, light, tiles, j, 0, rows, sems.at[len(copies)]))
    for copy in copies:
        copy.start()
    values[NT] = jnp.zeros((T, T), BF16)
    for copy in copies:
        copy.wait()
    zero = jnp.zeros((QR, T), jnp.float32)
    body = lambda g, c: light_dots(tiles, lambda p: values[p], ids, places, 0, g * STEP, c)
    out[0], out[1] = lax.fori_loop(0, trips[0], body, [zero, zero])


def first_kernel(meta, trips, ids, places, hplaces, light, heavy, near, *rest):
    parts, (out, values, tiles, htiles, sems) = rest[: 2 * len(HELD)], rest[2 * len(HELD) :]
    owner = meta[3]
    rows = pl.ds(pl.multiple_of(meta[1] * QR, QR), QR)
    copies = feature_copies(meta, HELD, parts, values, sems)
    for j in range(NEAR_STEPS, NB):
        copies.append(light_copy(meta, light, tiles, j, NEAR_STEPS, rows, sems.at[len(copies)]))
    for slot in range(2):
        rows, span = pl.ds(slot * QR, QR), pl.ds(slot * NG, NG)
        copies.append(
            pltpu.make_async_copy(heavy.at[:, rows, :], htiles.at[span], sems.at[len(copies)])
        )
    for copy in copies:
        copy.start()
    values[NT] = jnp.zeros((T, T), BF16)
    for copy in copies:
        copy.wait()
    value = lambda p: values[p]
    body = lambda g, c: light_dots(tiles, value, ids, places, NEAR_STEPS, FAR_AT + g * STEP, c)
    sums = lax.fori_loop(0, trips[1], body, [near[0], near[1]])

    def heavy_body(g, acc):
        base = g * HSTEP
        return dots(
            lambda i: htiles[i], value, HSTEP,
            lambda u: base + u, lambda u: hplaces[base + u], acc,
        )

    hsum = lax.fori_loop(0, SLOTS // HSTEP, heavy_body, jnp.zeros((QR, T), jnp.float32))
    for t in range(2):
        total = (sums[t] + jnp.where(owner == t, hsum, 0.0)).astype(BF16)
        for n in range(2 * NR):
            out[n, t] = total


def project_kernel(across, n, meta, *refs):
    parts, (w_in, b_in, w_mid, mine, theirs) = refs[:n], refs[n:]
    y = meta[0] & 1
    at = 0
    for part, first in zip(parts, across):
        size = part.shape[0]
        for k in range(size):
            group = pl.ds(at + jnp.bitwise_xor(y, k + first) * NR, NR)
            x = part[k].reshape(-1, T)
            h = jnp.dot(x, w_in[...], preferred_element_type=jnp.float32) + b_in[...]
            h = jnp.maximum(h, 0.0).astype(BF16)
            s = jnp.dot(h, w_mid[...], preferred_element_type=jnp.float32).astype(BF16)
            s = s.reshape(NR, 2, 2, QR, 2 * T)
            for rt in range(2):
                mine[rt, group] = s[:, :, rt, :, :T]
                theirs[rt, group] = s[:, :, rt, :, T:]
        if size == 2:
            at += NPLANE


def value_copies(meta, held, parts, values, sems):
    copies = []
    for which in range(2):
        c = meta[2] if which == 0 else 1 - meta[2]
        for k, at, start, size in held:
            part = parts[which * (held[-1][0] + 1) + k]
            for rt in range(2):
                span = pl.ds(rt * NG + start, size)
                copies.append(
                    pltpu.make_async_copy(
                        part.at[rt, pl.ds(at, size)], values.at[span, :, c], sems.at[len(copies)]
                    )
                )
    return copies


def second_near_kernel(meta, trips, need, ids, places, light, *rest):
    parts, (out, values, tiles, sems, light_sems) = rest[:4], rest[4:]
    copies = value_copies(meta, PROJECTED[:3], parts, values, sems)
    chunks = [light_copy(meta, light, tiles, j, 0, None, light_sems.at[j]) for j in range(NEAR_STEPS)]
    for copy in copies + chunks:
        copy.start()
    values[NT] = jnp.zeros((2, 2, QR, T), BF16)
    for copy in copies:
        copy.wait()

    def wait_for(n):
        span = pl.ds(n * LT, LT)
        pltpu.make_async_copy(light.at[span], tiles.at[span], light_sems.at[n]).wait()
        return n + 1

    value = lambda p: values[p].reshape(T, T)

    def body(g, carry):
        here = lax.while_loop(lambda n: n <= need[g], wait_for, carry[2])
        return (*light_dots(tiles, value, ids, places, 0, g * STEP, carry[:2]), here)

    zero = jnp.zeros((T, T), jnp.float32)
    sum0, sum1, here = lax.fori_loop(0, trips[0], body, (zero, zero, 0))
    lax.while_loop(lambda n: n < NEAR_STEPS, wait_for, here)
    out[0] = sum0
    out[1] = sum1


def second_kernel(
    meta, trips, htrips, ids, places, hids, hplaces, light, h0, h1, h2, h3, near, b_mid, *rest
):
    parts, (out, values, tiles, htiles, sems) = rest[:6], rest[6:]
    feat, owner = meta[1], meta[3]
    copies = value_copies(meta, PROJECTED, parts, values, sems)
    for j in range(NEAR_STEPS, NB):
        copies.append(light_copy(meta, light, tiles, j, NEAR_STEPS, None, sems.at[len(copies)]))
    first = len(copies)
    for k, h in enumerate((h0, h1, h2, h3)):
        rows = pl.ds(pl.multiple_of((feat ^ k) * QR, QR), QR)
        for slot in range(2):
            copies.append(
                pltpu.make_async_copy(
                    h.at[:, pl.ds(slot * QR, QR), :],
                    htiles.at[pl.ds(slot * NG, NG), rows, :],
                    sems.at[len(copies)],
                )
            )
    for copy in copies:
        copy.start()
    values[NT] = jnp.zeros((2, 2, QR, T), BF16)
    for copy in copies[:first]:
        copy.wait()
    value = lambda p: values[p].reshape(T, T)
    body = lambda g, c: light_dots(tiles, value, ids, places, NEAR_STEPS, FAR_AT + g * STEP, c)
    sums = lax.fori_loop(0, trips[1], body, [near[0], near[1]])
    for copy in copies[first:]:
        copy.wait()

    def heavy_body(g, acc):
        base = g * HLIST_STEP
        return dots(
            lambda i: htiles[i], value, HLIST_STEP, lambda u: hids[base + u], lambda u: hplaces[base + u], acc
        )

    hsum = lax.fori_loop(0, htrips[0], heavy_body, jnp.zeros((T, T), jnp.float32))
    for t in range(2):
        total = sums[t] + jnp.where(owner == t, hsum, 0.0) + b_mid[...]
        out[t * T : (t + 1) * T] = total.astype(BF16)


def per_device(
    features, weight_in, bias_in, weight_mid, bias_mid, light_tiles, light_rows, light_cols,
    heavy_tiles, heavy_slots, heavy_cols, owner_map,
):
    i32 = jnp.int32
    blk, core, feat = lax.axis_index(BLK), lax.axis_index("c"), lax.axis_index(FEAT)
    meta = jnp.stack([blk, feat, core, owner_map[0]]).astype(i32)
    in_hbm = lambda x: pltpu.with_memory_space_constraint(x, pltpu.MemorySpace.HBM)
    light = in_hbm(light_tiles.reshape(NL, T, T))
    int_list = jax.ShapeDtypeStruct((NL,), i32)
    int_lists = jax.ShapeDtypeStruct((2, LIST), i32)
    needs = jax.ShapeDtypeStruct((FAR_AT // STEP,), i32)
    one_int = jax.ShapeDtypeStruct((1,), i32)
    two_ints = jax.ShapeDtypeStruct((2,), i32)

    half = lax.dynamic_slice_in_dim(features, core * T, T, axis=0)
    plane = everyone(half, PLANE, NPLANE)

    packed, ids, places, need, trips = pl.pallas_call(
        pack_kernel,
        out_shape=(
            jax.ShapeDtypeStruct((NG, 2 * QR + NOTES, T), BF16), int_lists, int_lists, needs, two_ints
        ),
        in_specs=[SMEM] * 5 + [HBM],
        out_specs=(VMEM, SMEM, SMEM, SMEM, SMEM),
        scratch_shapes=[
            pltpu.VMEM((NH + 1, QR, T), BF16),
            pltpu.SMEM((SLOTS,), i32),
            pltpu.SMEM((NG,), i32),
            pltpu.SemaphoreType.DMA(()),
        ],
        compiler_params=params(16),
        cost_estimate=pl.CostEstimate(flops=0, transcendentals=0, bytes_accessed=30_000_000),
        name="pack",
    )(meta, heavy_slots, heavy_cols, light_rows, light_cols, in_hbm(heavy_tiles.reshape(NH, T, T)))
    arrived = lax.all_to_all(packed, GROUP, 0, 0, tiled=True)
    own = along_x(plane)
    own, far_parts = own[:3], own[3:]
    other = [swap(part, "c") for part in own]

    nodes = arrived[:, 2 * QR, :2].T.reshape(SLOTS).astype(i32)
    hplaces = jnp.where(
        nodes < NT, (nodes & 1) * NG + turned(blk, nodes >> 4) * NR + ((nodes & 15) >> 1), NT
    )

    trips, hplaces = lax.optimization_barrier((trips, hplaces))
    first_near = pl.pallas_call(
        first_near_kernel,
        out_shape=jax.ShapeDtypeStruct((2, QR, T), jnp.float32),
        in_specs=[SMEM] * 4 + [HBM] + [ANY] * 6,
        out_specs=VMEM,
        scratch_shapes=[
            pltpu.VMEM((NT + 1, T, T), BF16),
            pltpu.VMEM((NEAR_STEPS * LT, QR, T), BF16),
            pltpu.SemaphoreType.DMA((6 + NEAR_STEPS,)),
        ],
        compiler_params=params(10),
        name="first_near",
    )(meta, trips, ids, places, light, *own, *other)
    first_near, far_parts = lax.optimization_barrier((first_near, far_parts))
    held = own + far_parts + other + [swap(part, "c") for part in far_parts]
    aggregated = pl.pallas_call(
        first_kernel,
        out_shape=jax.ShapeDtypeStruct((2 * NR, 2, QR, T), BF16),
        in_specs=[SMEM] * 5 + [HBM, ANY, VMEM] + [ANY] * len(held),
        out_specs=VMEM,
        scratch_shapes=[
            pltpu.VMEM((NT + 1, T, T), BF16),
            pltpu.VMEM(((NB - NEAR_STEPS) * LT, QR, T), BF16),
            pltpu.VMEM((SLOTS, QR, T), BF16),
            pltpu.SemaphoreType.DMA((len(held) + 4,)),
        ],
        compiler_params=params(10),
        name="first",
    )(meta, trips, ids, places, hplaces, light, arrived, first_near, *held)

    aggregated, weight_in, bias_in, weight_mid = lax.optimization_barrier(
        (aggregated, weight_in, bias_in, weight_mid)
    )
    bias_rows = jnp.pad(bias_in.reshape(1, T), ((0, 7), (0, 0)))
    pieces = jnp.concatenate([weight_in.astype(jnp.float32), bias_rows], axis=0)
    pieces = jnp.stack([pieces, swap(pieces, "yl")])
    pieces = jnp.stack([pieces, swap(pieces, "c")], axis=1).reshape(4, T + 8, T)
    pieces = jnp.take(pieces, feat ^ jnp.arange(4), axis=0)
    w_in = jnp.moveaxis(pieces[:, :T], 0, 1).reshape(T, 4 * T).astype(BF16)
    b_in = pieces[:, T].reshape(1, 4 * T)
    w_mid = jnp.concatenate([weight_mid, swap(weight_mid, "c")], axis=1)

    column = lax.all_to_all(aggregated, ("z", "yl"), 0, 0, tiled=True).reshape(NR, 2, 2, QR, T)
    rows = jnp.stack([column, swap(column, "yh")])

    hids, hlist, htrips = pl.pallas_call(
        compact_kernel,
        out_shape=(int_list, int_list, one_int),
        in_specs=[SMEM],
        out_specs=(SMEM,) * 3,
        name="compact",
    )(hplaces)

    rows, arrived, w_in, b_in, w_mid, hids, hlist, htrips = lax.optimization_barrier(
        (rows, arrived, w_in, b_in, w_mid, hids, hlist, htrips)
    )
    hc = swap(arrived, "c")
    hy = swap(arrived, "yl")
    def project(parts, across):
        groups = sum(part.shape[0] for part in parts) * NR
        half_values = jax.ShapeDtypeStruct((2, groups, 2, QR, T), BF16)
        return pl.pallas_call(
            functools.partial(project_kernel, across, len(parts)),
            out_shape=(half_values, half_values),
            in_specs=[SMEM] + [VMEM] * (len(parts) + 3),
            out_specs=(VMEM, VMEM),
            compiler_params=params(12),
            name="project",
        )(meta, *parts, w_in, b_in, w_mid)

    behind = lax.ppermute(rows, "x", around("x", 1))
    ahead = lax.ppermute(rows, "x", around("x", -1))
    near = project([rows], (0,))
    behind, ahead, near = lax.optimization_barrier((behind, ahead, near))
    far = [
        lax.ppermute(behind[:1], "x", around("x", 1)),
        lax.ppermute(ahead[1:], "x", around("x", -1)),
    ]
    sides = project([behind, ahead], (0, 0))
    mine = [near[0], sides[0]]
    swapped = [swap(near[1], "c"), swap(sides[1], "c")]
    second_near = pl.pallas_call(
        second_near_kernel,
        out_shape=jax.ShapeDtypeStruct((2, T, T), jnp.float32),
        in_specs=[SMEM] * 5 + [HBM] + [ANY] * 4,
        out_specs=VMEM,
        scratch_shapes=[
            pltpu.VMEM((NT + 1, 2, 2, QR, T), BF16),
            pltpu.VMEM((NEAR_STEPS * LT, T, T), BF16),
            pltpu.SemaphoreType.DMA((12,)),
            pltpu.SemaphoreType.DMA((NEAR_STEPS,)),
        ],
        compiler_params=params(16),
        name="second_near",
    )(meta, trips, need, ids, places, light, *mine, *swapped)
    far, second_near = lax.optimization_barrier((far, second_near))
    far = project(far, (0, 1))
    mine.append(far[0])
    swapped.append(swap(far[1], "c"))
    hy_late, _ = lax.optimization_barrier((hy, far))
    hyc = swap(hy_late, "c")
    return pl.pallas_call(
        second_kernel,
        out_shape=jax.ShapeDtypeStruct((2 * T, T), BF16),
        in_specs=[SMEM] * 7 + [HBM] + [ANY] * 4 + [VMEM] * 2 + [ANY] * 6,
        out_specs=VMEM,
        scratch_shapes=[
            pltpu.VMEM((NT + 1, 2, 2, QR, T), BF16),
            pltpu.VMEM(((NB - NEAR_STEPS) * LT, T, T), BF16),
            pltpu.VMEM((SLOTS, T, T), BF16),
            pltpu.SemaphoreType.DMA((26,)),
        ],
        compiler_params=params(16),
        name="second",
    )(
        meta, trips, htrips, ids, places, hids, hlist, light, arrived, hc, hy, hyc, second_near,
        bias_mid.reshape(1, T), *mine, *swapped,
    )


def solution(mesh):
    wide = Mesh(mesh.devices.reshape(4, 2, 8, 2, 2), ("x", "yh", "z", "yl", "c"))
    in_specs = (
        P(GROUP, None),
        P(None, FEAT),
        P(FEAT),
        P(None, FEAT),
        P(FEAT),
        P(GROUP, None, None, None, None),
        P(GROUP, None, None),
        P(GROUP, None, None),
        P(GROUP, None, None, None, None),
        P(GROUP, None, None),
        P(GROUP, None, None),
        P(GROUP),
    )
    return jax.shard_map(
        per_device, mesh=wide, in_specs=in_specs, out_specs=P(GROUP, FEAT), check_vma=False
    )
```
